256 devices in a mesh: pipe: 8 (over z), tp: 32 (over y, x, core).
Axes of the slice: x: 4, y: 4, z: 8, core: 2. Of those that a mesh axis runs over, the one named last changes fastest.
Arguments:
- x_prev: bfloat16 [8, 128, 12288], P('pipe', None, 'tp'), may hold values from -6 to 6
- x_saved: bfloat16 [8, 128, 12288], P('pipe', None, 'tp'), may hold values from -6 to 6
- g_next: bfloat16 [8, 128, 12288], P('pipe', None, 'tp'), may hold values from -6 to 6
- w_qkv: bfloat16 [8, 12288, 32, 384], P('pipe', None, 'tp'), may hold values from -0.0546875 to 0.0546875
- w_out: bfloat16 [8, 4096, 12288], P('pipe', 'tp'), may hold values from -0.09375 to 0.09375
- gain: float32 [8, 12288], P('pipe'), may hold values from 0.5 to 1.5
- doc_ids: int32 [8, 2, 128], P('pipe'), may hold values from 0 to 3, never falling along the last dimension, each value on 1 to 64 neighbouring positions
Outputs:
- y_out: bfloat16 [8, 128, 12288], P('pipe', None, 'tp')
- section_input_gradient: bfloat16 [8, 128, 12288], P('pipe', None, 'tp')
The draws below stay inside these ranges and needn't reach their ends.
Inputs may be any that keep to these rules, and one draw needn't show every extreme that they name: `doc_ids`: document ids never fall along a micro-batch; each document holds 1 to 64 tokens and one holds exactly that many.
All inputs are finite; a program needn't handle non-finite values.
Results may differ from the reference program's by a relative error of at most 0.019.
Values may be sent and summed in bfloat16 or wider, within the bound.
A program may use at most 128 MiB of HBM per device.

```python
import math
import jax
import jax.numpy as jnp
import numpy as np
from jax import lax

D = 12288
HEAD_DIM = 128
LENGTH = 128
DOCS = 4
HEADS = 32
N_PIPE = 8


def block_levels(key, dims, shards, low, largest):
    def one(dim, shards_of):
        heights = jax.random.uniform(jax.random.fold_in(jax.random.fold_in(key, 6), dim), (shards_of,), jnp.float32, low / len(shards), largest / len(shards))
        return jnp.repeat(jnp.exp(heights), dims[dim] // shards_of).reshape((-1,) + (1,) * (len(dims) - dim - 1))

    factor_of = one(*shards[0])
    for cut in shards[1:]:
        factor_of = factor_of * one(*cut)
    return factor_of


def length_profile(count, total, reach, skew):
    weights = [(1 << 20) // math.isqrt(standing ** skew) + 1 for standing in range(2, count + 1)]
    surplus, given = total - reach - (count - 1), [1] * (count - 1)
    while surplus > 0:
        movable = [i for i in range(count - 1) if given[i] < reach]
        whole, remaining = sum([weights[i] for i in movable]), surplus
        for i in movable:
            extra = min(reach - given[i], max(1, remaining * weights[i] // whole), surplus)
            given[i] = given[i] + extra
            surplus = surplus - extra
    return np.array([reach] + given)


def ragged_sizes(rng, number_of, total, most, lean):
    if number_of == 2:
        one = jax.random.randint(rng, (), max(1, total - most), min(most, total - 1) + 1)
        return jnp.stack([one, total - one])
    sizes = jnp.asarray(length_profile(number_of, total, most, lean), jnp.int32)
    pairs = (number_of - 1) // 2
    giver, sink = sizes[1:1 + 2 * pairs:2], sizes[2:2 + 2 * pairs:2]
    slack = jnp.minimum(giver - 1, most - sink)
    moved = jax.random.randint(jax.random.fold_in(rng, 1), (pairs,), 0, 1 << 20) % (slack + 1)
    sizes = sizes.at[1:1 + 2 * pairs:2].set(giver - moved).at[2:2 + 2 * pairs:2].set(sink + moved)
    return sizes[jax.random.permutation(jax.random.fold_in(rng, 2), number_of)]


def gaussian(key, dims, scale, most, split=(), kind=jnp.bfloat16):
    entries = scale * jax.random.normal(key, dims, jnp.float32)
    if split:
        entries = entries * block_levels(key, dims, split, -0.22, 0.18)
    return jnp.clip(entries, -most, most).astype(kind)


def setup_inputs(seed: int = 0) -> dict:
    key_list = jax.random.split(jax.random.key(seed), 8)
    x_prev = gaussian(key_list[0], (N_PIPE, LENGTH, D), 1.0, 6.0, ((0, 8), (2, 32)))
    x_saved = gaussian(key_list[1], (N_PIPE, LENGTH, D), 1.0, 6.0, ((0, 8), (2, 32)))
    g_next = gaussian(key_list[2], (N_PIPE, LENGTH, D), 1.0, 6.0, ((0, 8), (2, 32)))
    w_qkv = gaussian(key_list[3], (N_PIPE, D, HEADS, 3 * HEAD_DIM), D ** -0.5, 0.0546875, ((0, 8), (2, 32)))
    w_out = gaussian(key_list[4], (N_PIPE, HEADS * HEAD_DIM, D), (HEADS * HEAD_DIM) ** -0.5, 0.09375, ((0, 8), (1, 32)))
    gain = jnp.clip(0.5 + 1.0 * jax.random.uniform(key_list[5], (N_PIPE, D), jnp.float32) ** block_levels(key_list[5], (N_PIPE, D), ((0, 8),), -0.2, 0.2), 0.5, 1.5)
    doc_ids = jax.vmap(lambda own: jnp.searchsorted(jnp.cumsum(ragged_sizes(own, DOCS, LENGTH, LENGTH // 2, 0)), jnp.arange(LENGTH), side="right"))(jax.random.split(key_list[6], N_PIPE * 2)).reshape((N_PIPE, 2, LENGTH)).astype(jnp.int32)
    return {"x_prev": x_prev, "x_saved": x_saved, "g_next": g_next, "w_qkv": w_qkv, "w_out": w_out, "gain": gain, "doc_ids": doc_ids}


EPS = 1e-05

def layer_stats(inputs, gain_forward_copy):
    values = inputs.astype(jnp.float32)
    center = lax.optimization_barrier(jnp.mean(values, -1, keepdims=True))
    square = lax.optimization_barrier(jnp.mean(values * values, -1, keepdims=True))
    inv_std = lax.rsqrt(square - center * center + EPS)
    x_hat = (values - center) * inv_std
    return (x_hat, inv_std, (x_hat * gain_forward_copy).astype(jnp.bfloat16))

def build_mask(doc_row):
    positions = jnp.arange(doc_row.shape[0], dtype=jnp.int32)
    return (positions[None, :] <= positions[:, None]) & (doc_row[:, None] == doc_row[None, :])

def attend(queries, key_rows, value_rows, visible):
    scaling = 1.0 / math.sqrt(HEAD_DIM)
    scores = jnp.einsum('qhe,khe->hqk', queries.astype(jnp.float32), key_rows.astype(jnp.float32)) * scaling
    scores = jnp.where(visible[None], scores, -1e+30)
    highest = lax.optimization_barrier(jnp.max(scores, -1, keepdims=True))
    exponent = jnp.exp(scores - highest)
    attn_probs = exponent / lax.optimization_barrier(jnp.sum(exponent, -1, keepdims=True))
    probs_low = attn_probs.astype(jnp.bfloat16)
    mixed = jnp.einsum('hqk,khe->qhe', probs_low.astype(jnp.float32), value_rows.astype(jnp.float32))
    return (mixed.astype(jnp.bfloat16), attn_probs, probs_low)

def section(inputs):
    x_in, x_back, incoming_gradient, w_qkv, w_out, gain, doc_ids = inputs
    row_count = x_in.shape[0]
    head_cols = HEADS * HEAD_DIM
    gain_forward_copy = gain.astype(jnp.float32)
    w_flat = w_qkv.reshape(D, 3 * head_cols)
    x_hat, inv_std, hidden = layer_stats(x_in, gain_forward_copy)
    qkv_f = jnp.dot(hidden, w_flat, preferred_element_type=jnp.float32).astype(jnp.bfloat16)
    qkv_f = qkv_f.reshape(row_count, HEADS, 3, HEAD_DIM)
    mixed = attend(qkv_f[:, :, 0], qkv_f[:, :, 1], qkv_f[:, :, 2], build_mask(doc_ids[0]))[0]
    projected = jnp.dot(mixed.reshape(row_count, head_cols), w_out, preferred_element_type=jnp.float32)
    y_out = (x_in.astype(jnp.float32) + projected).astype(jnp.bfloat16)
    normed_input_backward, reciprocal_deviation_backward, hidden_b = layer_stats(x_back, gain_forward_copy)
    qkv_b = jnp.dot(hidden_b, w_flat, preferred_element_type=jnp.float32).astype(jnp.bfloat16)
    qkv_b = qkv_b.reshape(row_count, HEADS, 3, HEAD_DIM)
    queries, key_rows, value_rows = (qkv_b[:, :, 0], qkv_b[:, :, 1], qkv_b[:, :, 2])
    mixed_b, attn_probs, probs_low = attend(queries, key_rows, value_rows, build_mask(doc_ids[1]))
    d_out = jnp.dot(incoming_gradient, w_out.T, preferred_element_type=jnp.float32).astype(jnp.bfloat16)
    d_three = d_out.reshape(row_count, HEADS, HEAD_DIM).astype(jnp.float32)
    d_values = jnp.einsum('hqk,qhe->khe', probs_low.astype(jnp.float32), d_three).astype(jnp.bfloat16)
    d_probs = jnp.einsum('qhe,khe->hqk', d_three, value_rows.astype(jnp.float32))
    d_scores = (attn_probs * (d_probs - lax.optimization_barrier(jnp.sum(d_probs * attn_probs, -1, keepdims=True))) / math.sqrt(HEAD_DIM)).astype(jnp.bfloat16)
    d_scores = lax.optimization_barrier(d_scores).astype(jnp.float32)
    d_query = jnp.einsum('hqk,khe->qhe', d_scores, key_rows.astype(jnp.float32)).astype(jnp.bfloat16)
    d_keys = jnp.einsum('hqk,qhe->khe', d_scores, queries.astype(jnp.float32)).astype(jnp.bfloat16)
    d_qkv = jnp.stack([d_query, d_keys, d_values], 2).reshape(row_count, 3 * head_cols)
    hidden_gradient = jnp.dot(d_qkv, w_flat.T, preferred_element_type=jnp.float32)
    normed_input_gradient = hidden_gradient * gain_forward_copy
    gradient_average = lax.optimization_barrier(jnp.mean(normed_input_gradient, -1, keepdims=True))
    gradient_projected_dot = lax.optimization_barrier(jnp.mean(normed_input_gradient * normed_input_backward, -1, keepdims=True))
    section_input_gradient = (incoming_gradient.astype(jnp.float32) + reciprocal_deviation_backward * (normed_input_gradient - gradient_average - normed_input_backward * gradient_projected_dot)).astype(jnp.bfloat16)
    return (y_out, section_input_gradient)

def reference(x_prev, x_saved, g_next, w_qkv, w_out, gain, doc_ids):
    x_in = jnp.roll(x_prev, 1, 0)
    incoming_gradient = jnp.roll(g_next, -1, 0)
    y_out, section_input_gradient = lax.map(section, (x_in, x_saved, incoming_gradient, w_qkv, w_out, gain, doc_ids))
    return (y_out, section_input_gradient)
```

```python
import functools
import math

import jax
import jax.numpy as jnp
from jax import lax
from jax.experimental import pallas as pl
from jax.experimental.pallas import tpu as pltpu
from jax.sharding import PartitionSpec as P

D = 12288
HEAD_DIM = 128
EPS = 1e-05
ROWS = 128
WIDTH = 384
HALF = 64
QUARTER = 32
THREE = 3 * HEAD_DIM
SCALE = 1.0 / math.sqrt(HEAD_DIM)
MESH = pl.DeviceIdType.MESH
F32 = jnp.float32
BF16 = jnp.bfloat16
NT = (((1,), (1,)), ((), ()))
TN = (((0,), (0,)), ((), ()))
N_MESSAGES = 160

OFFSET = (0, 1, 3, 2)


def mm(a, b, dims=None):
    if dims is None:
        return jnp.dot(a, b, preferred_element_type=F32)
    return lax.dot_general(a, b, dims, preferred_element_type=F32)


class Wire:
    def __init__(self, send_sems, recv_sems):
        self.send_sems, self.recv_sems = send_sems, recv_sems
        self.count = 0
        self.open = []

    def send(self, src, dst, device):
        copy = pltpu.make_async_remote_copy(
            src_ref=src,
            dst_ref=dst,
            send_sem=self.send_sems.at[self.count],
            recv_sem=self.recv_sems.at[self.count],
            device_id=device,
            device_id_type=MESH,
        )
        self.count += 1
        copy.start()
        self.open.append(copy)
        return copy

    def drain(self):
        for copy in self.open:
            copy.wait_send()
        self.open = []


def wait_all(copies):
    for copy in copies:
        copy.wait_recv()


class Gather:
    def __init__(self, wire, near, slots):
        self.wire, self.near, self.slots = wire, near, slots

    def first(self, own):
        s, w, n = self.slots, self.wire, self.near
        a, b = pl.ds(0, HALF), pl.ds(HALF, HALF)
        self.one = [
            w.send(own.at[a], s.at[0, 2, a], n["xp"]),
            w.send(own.at[a], s.at[0, 1, a], n["xm"]),
            w.send(own.at[b], s.at[2, 0, b], n["yp"]),
            w.send(own.at[b], s.at[1, 0, b], n["ym"]),
        ]

    def second(self):
        s, w, n = self.slots, self.wire, self.near
        wait_all(self.one)
        a0, a1 = pl.ds(0, QUARTER), pl.ds(QUARTER, QUARTER)
        b0, b1 = pl.ds(HALF, QUARTER), pl.ds(HALF + QUARTER, QUARTER)
        self.two = [
            w.send(s.at[0, 2, a0], s.at[0, 3, a0], n["xp"]),
            w.send(s.at[0, 1, a1], s.at[0, 3, a1], n["xm"]),
            w.send(s.at[2, 0, b0], s.at[3, 0, b0], n["yp"]),
            w.send(s.at[1, 0, b1], s.at[3, 0, b1], n["ym"]),
        ]
        self.three = [self._across(pl.ds(0, 3)), None]

    def third(self):
        wait_all(self.two)
        self.three[1] = self._across(pl.ds(3, 1))

    def _across(self, part):
        s, w, n = self.slots, self.wire, self.near
        a, b = pl.ds(0, HALF), pl.ds(HALF, HALF)
        return [
            w.send(s.at[0, part, a], s.at[2, part, a], n["yp"]),
            w.send(s.at[0, part, a], s.at[1, part, a], n["ym"]),
            w.send(s.at[part, 0, b], s.at[part, 2, b], n["xp"]),
            w.send(s.at[part, 0, b], s.at[part, 1, b], n["xm"]),
        ]

    def fourth(self, which):
        s, w, n = self.slots, self.wire, self.near
        wait_all(self.three[which])
        part = (pl.ds(0, 3), pl.ds(3, 1))[which]
        a0, a1 = pl.ds(0, QUARTER), pl.ds(QUARTER, QUARTER)
        b0, b1 = pl.ds(HALF, QUARTER), pl.ds(HALF + QUARTER, QUARTER)
        copies = [
            w.send(s.at[2, part, a0], s.at[3, part, a0], n["yp"]),
            w.send(s.at[1, part, a1], s.at[3, part, a1], n["ym"]),
            w.send(s.at[part, 2, b0], s.at[part, 3, b0], n["xp"]),
            w.send(s.at[part, 1, b1], s.at[part, 3, b1], n["xm"]),
        ]
        if which == 0:
            self.four = copies
        else:
            self.four += copies

    def finish(self):
        wait_all(self.four)


def add_into(target, *terms):
    total = target[...].astype(F32)
    for term in terms:
        total = total + term[...].astype(F32)
    target[...] = total.astype(BF16)


class Scatter:
    def __init__(self, wire, near, parts, a1, a2, b1, b2):
        self.wire, self.near, self.parts = wire, near, parts
        self.a1, self.a2, self.b1, self.b2 = a1, a2, b1, b2

    def _long(self, half, pos, rows):
        rows = pl.ds(half * HALF + rows, QUARTER)
        if half == 0:
            return self.parts.at[pos, pl.ds(0, 4), rows]
        return self.parts.at[pl.ds(0, 4), pos, rows]

    def _short(self, half, pos, rows):
        rows = pl.ds(half * HALF + rows, QUARTER)
        if half == 0:
            return self.parts.at[0, pos, rows]
        return self.parts.at[pos, 0, rows]

    def _ways(self, half, long):
        axis = "y" if (half == 0) == long else "x"
        return self.near[axis + "p"], self.near[axis + "m"]

    def _start(self, half, view, r1, r2, long):
        up, down = self._ways(half, long)
        w, lead = self.wire, (pl.ds(0, 4),) if long else ()
        lo, hi = pl.ds(0, QUARTER), pl.ds(QUARTER, QUARTER)
        one = [
            w.send(view(half, 3, 0), r1.at[half, 0], up),
            w.send(view(half, 3, QUARTER), r1.at[half, 1], down),
        ]
        two = [
            w.send(view(half, 1, QUARTER), r2.at[(half, 0) + lead + (hi,)], up),
            w.send(view(half, 2, 0), r2.at[(half, 1) + lead + (lo,)], down),
        ]
        return one, two

    def _pass(self, half, view, r1, r2, long, one, two):
        up, down = self._ways(half, long)
        w, lead = self.wire, (pl.ds(0, 4),) if long else ()
        lo, hi = pl.ds(0, QUARTER), pl.ds(QUARTER, QUARTER)
        one[0].wait_recv()
        add_into(view(half, 1, 0), r1.at[half, 0])
        two.append(w.send(view(half, 1, 0), r2.at[(half, 0) + lead + (lo,)], up))
        one[1].wait_recv()
        add_into(view(half, 2, QUARTER), r1.at[half, 1])
        two.append(w.send(view(half, 2, QUARTER), r2.at[(half, 1) + lead + (hi,)], down))

    def first(self):
        self.long = [self._start(h, self._long, self.a1, self.a2, True) for h in (0, 1)]

    def second(self):
        for h in (0, 1):
            self._pass(h, self._long, self.a1, self.a2, True, *self.long[h])

    def third(self):
        self.short = []
        for h in (0, 1):
            wait_all(self.long[h][1])
            for pos in (3, 1, 2, 0):
                for q in (0, QUARTER):
                    rows = pl.ds(q, QUARTER)
                    add_into(
                        self._short(h, pos, q),
                        self.a2.at[h, 0, pos, rows],
                        self.a2.at[h, 1, pos, rows],
                    )
            self.short.append(self._start(h, self._short, self.b1, self.b2, False))

    def fourth(self):
        for h in (0, 1):
            self._pass(h, self._short, self.b1, self.b2, False, *self.short[h])

    def finish(self):
        halves = []
        for h in (0, 1):
            wait_all(self.short[h][1])
            own = self.parts[0, 0, pl.ds(h * HALF, HALF)].astype(F32)
            halves.append(own + self.b2[h, 0].astype(F32) + self.b2[h, 1].astype(F32))
        return jnp.concatenate(halves, axis=0)


def partial_sums(slots, sums):
    def body(i, carry):
        one, two = carry
        block = slots[i // 4, i % 4].astype(F32)
        for k in range(WIDTH // 128):
            part = block[:, k * 128 : (k + 1) * 128]
            one, two = one + part, two + part * part
        return one, two

    zero = jnp.zeros((ROWS, 128), F32)
    one, two = lax.fori_loop(0, 16, body, (zero, zero))
    sums[0] = one
    sums[1] = two


def statistics(mine, other):
    center = jnp.sum(mine[0] + other[0], -1, keepdims=True) * (1.0 / D)
    square = jnp.sum(mine[1] + other[1], -1, keepdims=True) * (1.0 / D)
    return center, lax.rsqrt(square - center * center + EPS)


def project(slots, gains, weights, total, center, inv_std, with_gain):
    def body(i, _):
        row, col = i // 2, (i % 2) * 2
        blocks = []
        for k in range(2):
            gain = gains[row, col + k]
            hidden = (slots[row, col + k].astype(F32) - center) * inv_std * gain
            block = hidden.astype(BF16)
            if with_gain:
                high = gain.astype(BF16).astype(F32)
                middle = (gain - high).astype(BF16).astype(F32)
                low = gain - high - middle
                at = lax.broadcasted_iota(jnp.int32, (16, WIDTH), 0)
                extra = jnp.where(at == 0, high, jnp.where(at == 1, middle, low))
                extra = jnp.where(at < 3, extra, 0.0)
                block = jnp.concatenate([block, extra.astype(BF16)], axis=0)
            blocks.append(block)
        lhs = jnp.concatenate(blocks, axis=1)
        rhs = weights[row, pl.ds(col, 2)].reshape(2 * WIDTH, 2 * THREE)
        value = mm(lhs, rhs)

        @pl.when(i == 0)
        def _():
            total[...] = value

        @pl.when(i > 0)
        def _():
            total[...] += value

        return 0

    lax.fori_loop(0, 8, body, 0)


def visible_pairs(documents):
    across = jnp.broadcast_to(documents, (ROWS, ROWS))
    down = across.T
    query = lax.broadcasted_iota(jnp.int32, (ROWS, ROWS), 0)
    key = lax.broadcasted_iota(jnp.int32, (ROWS, ROWS), 1)
    return (key <= query) & (across == down)


def probabilities(queries, keys, visible):
    scores = jnp.where(visible, mm(queries, keys, NT) * SCALE, -1e30)
    exponent = jnp.exp(scores - jnp.max(scores, -1, keepdims=True))
    return exponent / jnp.sum(exponent, -1, keepdims=True)


def kernel(
    x_prev, x_saved, g_next, w_qkv, w_out, gain, doc_ids,
    y_out, grad_out,
    sb, sg, sf, weights, w_o, gains, part_d, part_y,
    da1, da2, db1, db2, ya1, ya2, yb1, yb2,
    sums, sums_in, total_b, total_f, qkv_in, d_o, d_o_in, d_cat, o_cat,
    corr, corr_in,
    send_sems, recv_sems, local_sems, swap_send, swap_recv,
):
    z, t = lax.axis_index("pipe"), lax.axis_index("tp")
    core, x, y = t % 2, (t // 2) % 4, t // 8
    planes = lax.axis_size("pipe")

    def at(dy, dx):
        return (z, (((y + dy) % 4) * 4 + (x + dx) % 4) * 2 + core)

    partner = (z, t + 1 - 2 * core)
    above, below = ((z + 1) % planes, t), ((z + planes - 1) % planes, t)
    near = {"xp": at(0, 1), "xm": at(0, 3), "yp": at(1, 0), "ym": at(3, 0)}
    x_far, y_far = at(0, 2), at(2, 0)

    barrier = pltpu.get_barrier_semaphore()
    everyone = [partner, above, below, x_far, y_far, *near.values()]
    for device in everyone:
        pl.semaphore_signal(barrier, inc=1, device_id=device, device_id_type=MESH)
    pl.semaphore_wait(barrier, len(everyone))

    wire = Wire(send_sems, recv_sems)
    gb, gg, gf = (Gather(wire, near, slots) for slots in (sb, sg, sf))
    rd = Scatter(wire, near, part_d, da1, da2, db1, db2)
    ry = Scatter(wire, near, part_y, ya1, ya2, yb1, yb2)

    own_b = pltpu.make_async_copy(x_saved, sb.at[0, 0], local_sems.at[0])
    own_b.start()
    gb.first(x_saved)
    shift_g = wire.send(g_next, sg.at[0, 0], below)
    shift_f = wire.send(x_prev, sf.at[0, 0], above)
    own_cols, their_cols = pl.ds(0, THREE), pl.ds(THREE, THREE)
    own_rows, their_rows = pl.ds(0, HEAD_DIM), pl.ds(HEAD_DIM, HEAD_DIM)
    for py in range(4):
        for px in range(4):
            chip = ((y + OFFSET[py]) % 4) * 4 + (x + OFFSET[px]) % 4
            pltpu.make_async_copy(
                w_qkv.at[chip, core], weights.at[py, px, :, own_cols], local_sems.at[1]
            ).start()
            pltpu.make_async_remote_copy(
                src_ref=w_qkv.at[chip, 1 - core],
                dst_ref=weights.at[py, px, :, their_cols],
                send_sem=swap_send.at[0],
                recv_sem=swap_recv.at[0],
                device_id=partner,
                device_id_type=MESH,
            ).start()
            pltpu.make_async_copy(
                gain.at[chip * 2 + core], gains.at[py, px], local_sems.at[3]
            ).start()
    own_b.wait()

    gb.second()
    for py in range(4):
        for px in range(4):
            chip = ((y + OFFSET[py]) % 4) * 4 + (x + OFFSET[px]) % 4
            mine = pl.multiple_of((chip * 2 + core) * WIDTH, 128)
            theirs = pl.multiple_of((chip * 2 + 1 - core) * WIDTH, 128)
            pltpu.make_async_copy(
                w_out.at[:, pl.ds(mine, WIDTH)], w_o.at[py, px, own_rows], local_sems.at[2]
            ).start()
            pltpu.make_async_remote_copy(
                src_ref=w_out.at[:, pl.ds(theirs, WIDTH)],
                dst_ref=w_o.at[py, px, their_rows],
                send_sem=swap_send.at[1],
                recv_sem=swap_recv.at[1],
                device_id=partner,
                device_id_type=MESH,
            ).start()
    gb.third()
    shift_g.wait_recv()
    gg.first(sg.at[0, 0])
    gb.fourth(0)
    gg.second()
    gb.fourth(1)
    gg.third()
    shift_f.wait_recv()

    def swapped(ref, which):
        return pltpu.make_async_remote_copy(
            src_ref=ref,
            dst_ref=ref,
            send_sem=swap_send.at[which],
            recv_sem=swap_recv.at[which],
            device_id=partner,
            device_id_type=MESH,
        )

    gb.finish()
    partial_sums(sb, sums.at[0])
    stats = wire.send(sums.at[0], sums_in.at[0], partner)
    gf.first(sf.at[0, 0])
    pltpu.make_async_copy(gains, gains, local_sems.at[3]).wait()
    half_w = weights.at[:, :, :, own_cols]
    pltpu.make_async_copy(half_w, half_w, local_sems.at[1]).wait()
    swap_w = swapped(weights.at[:, :, :, their_cols], 0)
    swap_w.wait_recv()
    stats.wait_recv()
    center_b, inv_std_b = statistics(sums[0], sums_in[0])
    project(sb, gains, weights, total_b, center_b, inv_std_b, True)
    trade = wire.send(total_b.at[pl.ds(0, ROWS), their_cols], qkv_in.at[0], partner)
    gg.fourth(0)
    gg.fourth(1)
    gf.second()
    trade.wait_recv()
    qkv_b = total_b[pl.ds(0, ROWS), own_cols] + qkv_in[0]
    low_b = qkv_b.astype(BF16)
    queries, keys, values = (low_b[:, k * HEAD_DIM : (k + 1) * HEAD_DIM] for k in range(3))
    probs = probabilities(queries, keys, visible_pairs(doc_ids[pl.ds(1, 1)]))
    probs_low = probs.astype(BF16)
    gf.third()

    gg.finish()
    half_o = w_o.at[:, :, own_rows]
    pltpu.make_async_copy(half_o, half_o, local_sems.at[2]).wait()
    swap_o = swapped(w_o.at[:, :, their_rows], 1)
    swap_o.wait_recv()

    def output_gradient(i, total):
        row, col = i // 2, (i % 2) * 2
        lhs = jnp.concatenate([sg[row, col], sg[row, col + 1]], axis=1)
        rhs = jnp.concatenate([w_o[row, col], w_o[row, col + 1]], axis=1)
        return total + mm(lhs, rhs, NT)

    d_o[...] = lax.fori_loop(0, 8, output_gradient, jnp.zeros((ROWS, 2 * HEAD_DIM), F32))
    trade = wire.send(d_o.at[:, their_rows], d_o_in, partner)
    gf.fourth(0)
    gf.fourth(1)
    trade.wait_recv()
    d_low = (d_o[:, own_rows] + d_o_in[...]).astype(BF16)
    d_values = mm(probs_low, d_low, TN).astype(BF16)
    d_probs = mm(d_low, values, NT)
    d_scores = probs * (d_probs - jnp.sum(d_probs * probs, -1, keepdims=True)) * SCALE
    d_scores = d_scores.astype(BF16)
    d_queries = mm(d_scores, keys).astype(BF16)
    d_keys = mm(d_scores, queries, TN).astype(BF16)
    d_own = jnp.concatenate([d_queries, d_keys, d_values], axis=1)
    d_cat[:, own_cols] = d_own
    trade = wire.send(d_cat.at[:, own_cols], d_cat.at[:, their_cols], partner)
    along_qkv = jnp.sum(d_own.astype(F32) * qkv_b, -1, keepdims=True)
    trade.wait_recv()

    d_all = d_cat[...]
    for py, px in ((3, 0), (3, 2), (0, 2), (1, 2), (2, 2), (1, 0), (2, 0), (0, 0)):
        rhs = weights[py, pl.ds(px, 2)].reshape(2 * WIDTH, 2 * THREE)
        value = mm(d_all, rhs, NT).astype(BF16)
        part_d[py, px] = value[:, :WIDTH]
        part_d[py, px + 1] = value[:, WIDTH:]
    rd.first()

    gain_w = jnp.sum(total_b[pl.ds(ROWS, 8)], 0, keepdims=True)
    along_gain = jnp.sum(d_all.astype(F32) * gain_w, -1, keepdims=True)
    lane = lax.broadcasted_iota(jnp.int32, (ROWS, 128), 1)
    both = jnp.where(lane == 0, along_gain, jnp.where(lane == 1, along_qkv, 0.0))
    corr[0] = both.T[:8]
    corr_copy = wire.send(corr.at[0], corr_in.at[0], partner)

    gf.finish()
    partial_sums(sf, sums.at[1])
    stats = wire.send(sums.at[1], sums_in.at[1], partner)
    corr_copy.wait_recv()
    corr[1] = corr[0] + corr_in[0]
    corr_copies = [
        wire.send(corr.at[1], corr_in.at[k + 1], device)
        for k, device in enumerate((near["xp"], near["xm"], x_far))
    ]
    stats.wait_recv()
    center_f, inv_std_f = statistics(sums[1], sums_in[1])
    project(sf, gains, weights, total_f, center_f, inv_std_f, False)
    trade = wire.send(total_f.at[:, their_cols], qkv_in.at[1], partner)
    rd.second()
    wait_all(corr_copies)
    corr[2] = corr[1] + corr_in[1] + corr_in[2] + corr_in[3]
    corr_copies = [
        wire.send(corr.at[2], corr_in.at[k + 4], device)
        for k, device in enumerate((near["yp"], near["ym"], y_far))
    ]
    trade.wait_recv()
    low_f = (total_f[:, own_cols] + qkv_in[1]).astype(BF16)
    queries, keys, values = (low_f[:, k * HEAD_DIM : (k + 1) * HEAD_DIM] for k in range(3))
    probs = probabilities(queries, keys, visible_pairs(doc_ids[pl.ds(0, 1)]))
    o_cat[:, own_rows] = mm(probs.astype(BF16), values).astype(BF16)
    trade = wire.send(o_cat.at[:, own_rows], o_cat.at[:, their_rows], partner)
    trade.wait_recv()
    o_all = o_cat[...]
    for py, px in ((3, 0), (3, 2), (0, 2), (1, 2), (2, 2), (1, 0), (2, 0), (0, 0)):
        rhs = jnp.concatenate([w_o[py, px], w_o[py, px + 1]], axis=1)
        value = mm(o_all, rhs).astype(BF16)
        part_y[py, px] = value[:, :WIDTH]
        part_y[py, px + 1] = value[:, WIDTH:]
    ry.first()

    rd.third()
    ry.second()
    rd.fourth()
    ry.third()
    wait_all(corr_copies)
    corr[3] = corr[2] + corr_in[4] + corr_in[5] + corr_in[6]
    square = jnp.concatenate([corr[3], jnp.zeros((ROWS - 8, 128), F32)], axis=0).T
    mean_d, mean_dx = square[:, 0:1] * (1.0 / D), square[:, 1:2] * (1.0 / D)
    hidden_gradient = rd.finish()
    x_hat = (sb[0, 0].astype(F32) - center_b) * inv_std_b
    terms = hidden_gradient * gains[0, 0] - mean_d - x_hat * mean_dx
    grad_out[...] = (sg[0, 0].astype(F32) + inv_std_b * terms).astype(BF16)
    ry.fourth()
    swap_w.wait_send()
    swap_o.wait_send()
    y_out[...] = (sf[0, 0].astype(F32) + ry.finish()).astype(BF16)
    wire.drain()


def shards(x_prev, x_saved, g_next, w_qkv, w_out, gain, doc_ids):
    block = (ROWS, WIDTH)
    grid = (4, 4)
    any_spec = pl.BlockSpec(memory_space=pl.ANY)
    vmem_spec = pl.BlockSpec(memory_space=pltpu.VMEM)
    scatter_space = [
        pltpu.VMEM((2, 2, 4, QUARTER, WIDTH), BF16),
        pltpu.VMEM((2, 2, 4, HALF, WIDTH), BF16),
        pltpu.VMEM((2, 2, QUARTER, WIDTH), BF16),
        pltpu.VMEM((2, 2, HALF, WIDTH), BF16),
    ]
    y_out, grad = pl.pallas_call(
        kernel,
        out_shape=[jax.ShapeDtypeStruct(block, BF16)] * 2,
        in_specs=[any_spec] * 6 + [vmem_spec],
        out_specs=[vmem_spec] * 2,
        scratch_shapes=[
            *[pltpu.VMEM(grid + block, BF16)] * 3,
            pltpu.VMEM(grid + (WIDTH, 2 * THREE), BF16),
            pltpu.VMEM(grid + (2 * HEAD_DIM, WIDTH), BF16),
            pltpu.VMEM(grid + (1, WIDTH), F32),
            *[pltpu.VMEM(grid + block, BF16)] * 2,
            *scatter_space,
            *scatter_space,
            pltpu.VMEM((2, 2, ROWS, 128), F32),
            pltpu.VMEM((2, 2, ROWS, 128), F32),
            pltpu.VMEM((ROWS + 16, 2 * THREE), F32),
            pltpu.VMEM((ROWS, 2 * THREE), F32),
            pltpu.VMEM((2, ROWS, THREE), F32),
            pltpu.VMEM((ROWS, 2 * HEAD_DIM), F32),
            pltpu.VMEM((ROWS, HEAD_DIM), F32),
            pltpu.VMEM((ROWS, 2 * THREE), BF16),
            pltpu.VMEM((ROWS, 2 * HEAD_DIM), BF16),
            pltpu.VMEM((4, 8, 128), F32),
            pltpu.VMEM((7, 8, 128), F32),
            pltpu.SemaphoreType.DMA((N_MESSAGES,)),
            pltpu.SemaphoreType.DMA((N_MESSAGES,)),
            pltpu.SemaphoreType.DMA((4,)),
            pltpu.SemaphoreType.DMA((2,)),
            pltpu.SemaphoreType.DMA((2,)),
        ],
        compiler_params=pltpu.CompilerParams(
            collective_id=0, has_side_effects=True, vmem_limit_bytes=56 * 2**20
        ),
        name="section",
    )(
        x_prev[0],
        x_saved[0],
        g_next[0],
        w_qkv.reshape(16, 2, WIDTH, THREE),
        w_out[0],
        gain.reshape(32, 1, WIDTH),
        doc_ids[0],
    )
    return y_out[None], grad[None]


def solution(mesh):
    in_specs = (
        P("pipe", None, "tp"),
        P("pipe", None, "tp"),
        P("pipe", None, "tp"),
        P("pipe", None, "tp", None),
        P("pipe", "tp", None),
        P("pipe", None),
        P("pipe", None, None),
    )
    out_specs = (P("pipe", None, "tp"), P("pipe", None, "tp"))
    return jax.shard_map(shards, mesh=mesh, in_specs=in_specs, out_specs=out_specs, check_vma=False)
```

```python
import functools
import math

import jax
import jax.numpy as jnp
from jax import lax
from jax.experimental import pallas as pl
from jax.experimental.pallas import tpu as pltpu
from jax.sharding import PartitionSpec as P

D = 12288
HEAD_DIM = 128
EPS = 1e-05
ROWS = 128
WIDTH = 384
HALF = 64
QUARTER = 32
THREE = 3 * HEAD_DIM
SCALE = 1.0 / math.sqrt(HEAD_DIM)
MESH = pl.DeviceIdType.MESH
F32 = jnp.float32
BF16 = jnp.bfloat16
NT = (((1,), (1,)), ((), ()))
TN = (((0,), (0,)), ((), ()))
N_SENDERS, N_RECEIVERS = 20, 46

OFFSET = (0, 1, 3, 2)


def mm(a, b, dims=None):
    if dims is None:
        return jnp.dot(a, b, preferred_element_type=F32)
    return lax.dot_general(a, b, dims, preferred_element_type=F32)


class Wire:
    def __init__(self, send_sems, recv_sems, partner):
        self.send_sems, self.recv_sems, self.partner = send_sems, recv_sems, partner
        self.sends = self.receives = 0

    def sender(self):
        self.sends += 1
        return self.send_sems.at[self.sends - 1]

    def group(self, send_sem=None):
        self.receives += 1
        receiver = self.recv_sems.at[self.receives - 1]
        return Group(self.sender() if send_sem is None else send_sem, receiver, self.partner)

    def send(self, src, dst, device):
        group = self.group()
        group.send(src, dst, device)
        return group


class Group:
    def __init__(self, send_sem, recv_sem, partner):
        self.send_sem, self.recv_sem, self.partner = send_sem, recv_sem, partner

    def _copy(self, src, dst, device):
        return pltpu.make_async_remote_copy(
            src_ref=src,
            dst_ref=dst,
            send_sem=self.send_sem,
            recv_sem=self.recv_sem,
            device_id=device,
            device_id_type=MESH,
        )

    def send(self, src, dst, device):
        self.last = self._copy(src, dst, device)
        self.last.start()

    def received(self, like=None):
        (self.last if like is None else self._copy(like, like, self.partner)).wait_recv()

    def sent(self, like=None):
        (self.last if like is None else self._copy(like, like, self.partner)).wait_send()


class Gather:
    def __init__(self, wire, near, slots):
        self.near, self.slots = near, slots
        self.sender = wire.sender()
        self.one, self.two, self.three, self.more, self.four = (
            wire.group(self.sender) for _ in range(5)
        )

    def first(self, own):
        s, n, g = self.slots, self.near, self.one
        a, b = pl.ds(0, HALF), pl.ds(HALF, HALF)
        g.send(own.at[a], s.at[0, 2, a], n["xp"])
        g.send(own.at[b], s.at[2, 0, b], n["yp"])
        g.send(own.at[a], s.at[0, 1, a], n["xm"])
        g.send(own.at[b], s.at[1, 0, b], n["ym"])

    def second(self):
        s, n, g = self.slots, self.near, self.two
        self.one.received(s.at[0, pl.ds(0, 2)])
        a0, a1 = pl.ds(0, QUARTER), pl.ds(QUARTER, QUARTER)
        b0, b1 = pl.ds(HALF, QUARTER), pl.ds(HALF + QUARTER, QUARTER)
        g.send(s.at[0, 2, a0], s.at[0, 3, a0], n["xp"])
        g.send(s.at[2, 0, b0], s.at[3, 0, b0], n["yp"])
        g.send(s.at[0, 1, a1], s.at[0, 3, a1], n["xm"])
        g.send(s.at[1, 0, b1], s.at[3, 0, b1], n["ym"])
        self._across(self.three, pl.ds(0, 3))

    def third(self):
        self.two.received(self.slots.at[0, 0])
        self._across(self.more, pl.ds(3, 1))

    def _across(self, g, part):
        s, n = self.slots, self.near
        a, b = pl.ds(0, HALF), pl.ds(HALF, HALF)
        g.send(s.at[0, part, a], s.at[2, part, a], n["yp"])
        g.send(s.at[part, 0, b], s.at[part, 2, b], n["xp"])
        g.send(s.at[0, part, a], s.at[1, part, a], n["ym"])
        g.send(s.at[part, 0, b], s.at[part, 1, b], n["xm"])

    def _onward(self, part):
        s, n, g = self.slots, self.near, self.four
        a0, a1 = pl.ds(0, QUARTER), pl.ds(QUARTER, QUARTER)
        b0, b1 = pl.ds(HALF, QUARTER), pl.ds(HALF + QUARTER, QUARTER)
        g.send(s.at[2, part, a0], s.at[3, part, a0], n["yp"])
        g.send(s.at[part, 2, b0], s.at[part, 3, b0], n["xp"])
        g.send(s.at[1, part, a1], s.at[3, part, a1], n["ym"])
        g.send(s.at[part, 1, b1], s.at[part, 3, b1], n["xm"])

    def fourth(self):
        self.three.received(self.slots.at[pl.ds(0, 3), pl.ds(0, 2)])
        self._onward(pl.ds(0, 3))

    def fifth(self):
        self.more.received(self.slots.at[0, pl.ds(0, 2)])
        self._onward(pl.ds(3, 1))

    def finish(self):
        self.four.received(self.slots.at[0])


def add_into(target, *terms):
    total = target[...].astype(F32)
    for term in terms:
        total = total + term[...].astype(F32)
    target[...] = total.astype(BF16)


PIECES = ((3, 1), (1, 2), (0, 1))


class Scatter:
    def __init__(self, wire, near, parts, a1, a2, b1, b2):
        self.near, self.parts = near, parts
        self.a1, self.a2, self.b1, self.b2 = a1, a2, b1, b2
        self.sender = wire.sender()
        self.one = [wire.group(self.sender) for _ in range(4)]
        self.two = [wire.group(self.sender) for _ in range(4)]

    def _part(self, half, pos, rows, k):
        rows = pl.ds(half * HALF + rows, QUARTER)
        if k < 3:
            first, second = pos, pl.ds(*PIECES[k])
        else:
            first, second = 0, pos
        return self.parts.at[(first, second, rows) if half == 0 else (second, first, rows)]

    def _box(self, half, way, rows, k):
        rows = pl.ds(rows, QUARTER)
        if k < 3:
            piece = pl.ds(*PIECES[k])
            return self.a1.at[half, way, piece], self.a2.at[half, way, piece, rows]
        return self.b1.at[half, way], self.b2.at[half, way, rows]

    def _ways(self, half, k):
        axis = "y" if (half == 0) == (k < 3) else "x"
        return self.near[axis + "p"], self.near[axis + "m"]

    def far(self, k, half):
        for way, device in enumerate(self._ways(half, k)):
            self.one[k].send(
                self._part(half, 3, way * QUARTER, k), self._box(half, way, 0, k)[0], device
            )

    def close(self, k, half):
        for way, device in enumerate(self._ways(half, k)):
            rows = (1 - way) * QUARTER
            self.two[k].send(
                self._part(half, 1 + way, rows, k), self._box(half, way, rows, k)[1], device
            )

    def _pass(self, k):
        for half in (0, 1):
            for way, device in enumerate(self._ways(half, k)):
                part = self._part(half, 1 + way, way * QUARTER, k)
                add_into(part, self._box(half, way, 0, k)[0])
                self.two[k].send(part, self._box(half, way, way * QUARTER, k)[1], device)

    def _fold(self, half, pos):
        for q in (0, QUARTER):
            rows = pl.ds(q, QUARTER)
            add_into(
                self._part(half, pos, q, 3),
                self.a2.at[half, 0, pos, rows],
                self.a2.at[half, 1, pos, rows],
            )

    def second(self, k):
        self.one[k].received(self.parts.at[0, pl.ds(0, PIECES[k][1])])
        self._pass(k)

    def third(self):
        self.two[0].received(self.parts.at[0, pl.ds(0, 2)])
        for half in (0, 1):
            self._fold(half, 3)
            self.far(3, half)

    def fourth(self):
        self.two[1].received(self.parts.at[0])
        for half in (0, 1):
            self._fold(half, 1)
            self._fold(half, 2)
            self.close(3, half)

    def fifth(self):
        self.one[3].received(self.parts.at[0, 0])
        self._pass(3)

    def finish(self):
        self.two[2].received(self.parts.at[0, pl.ds(0, 2)])
        self.two[3].received(self.parts.at[0, pl.ds(0, 2)])
        halves = []
        for half in (0, 1):
            total = self.parts[0, 0, pl.ds(half * HALF, HALF)].astype(F32)
            for term in (
                self.a2[half, 0, 0], self.a2[half, 1, 0], self.b2[half, 0], self.b2[half, 1]
            ):
                total = total + term.astype(F32)
            halves.append(total)
        return jnp.concatenate(halves, axis=0)


class AllSum:
    def __init__(self, wire, partner, along_x, along_y, held, box):
        self.held, self.box, self.partner, self.x, self.y = held, box, partner, along_x, along_y
        self.groups = [wire.group() for _ in range(3)]

    def start(self, columns):
        lane = lax.broadcasted_iota(jnp.int32, (ROWS, 128), 1)
        square = jnp.zeros((ROWS, 128), F32)
        for k, column in enumerate(columns):
            square = jnp.where(lane == k, column, square)
        self.held[0] = square.T[:8]
        self.groups[0].send(self.held.at[0], self.box.at[0], self.partner)

    def along_x(self):
        self.groups[0].received()
        self.held[1] = self.held[0] + self.box[0]
        for k, device in enumerate(self.x):
            self.groups[1].send(self.held.at[1], self.box.at[1 + k], device)

    def along_y(self):
        self.groups[1].received(self.box.at[pl.ds(1, 3)])
        self.held[2] = self.held[1] + self.box[1] + self.box[2] + self.box[3]
        for k, device in enumerate(self.y):
            self.groups[2].send(self.held.at[2], self.box.at[4 + k], device)

    def columns(self, count):
        self.groups[2].received(self.box.at[pl.ds(4, 3)])
        total = self.held[2] + self.box[4] + self.box[5] + self.box[6]
        square = jnp.concatenate([total, jnp.zeros((ROWS - 8, 128), F32)], axis=0).T
        return [square[:, k : k + 1] for k in range(count)]

    def sent(self):
        self.groups[0].sent()
        self.groups[1].sent(self.box.at[pl.ds(1, 3)])
        self.groups[2].sent(self.box.at[pl.ds(4, 3)])


def own_sums(block):
    values = block.astype(F32)
    return [jnp.sum(v, -1, keepdims=True) for v in (values, values * values)]


def statistics(total, square):
    center = total * (1.0 / D)
    return center, lax.rsqrt(square * (1.0 / D) - center * center + EPS)


def project(slots, gains, weights, total, center, inv_std, with_gain, first, last):
    def body(i, _):
        row, col = i // 2, (i % 2) * 2
        blocks = []
        for k in range(2):
            gain = gains[row, col + k]
            hidden = (slots[row, col + k].astype(F32) - center) * inv_std * gain
            block = hidden.astype(BF16)
            if with_gain:
                high = gain.astype(BF16).astype(F32)
                middle = (gain - high).astype(BF16).astype(F32)
                low = gain - high - middle
                at = lax.broadcasted_iota(jnp.int32, (16, WIDTH), 0)
                extra = jnp.where(at == 0, high, jnp.where(at == 1, middle, low))
                extra = jnp.where(at < 3, extra, 0.0)
                block = jnp.concatenate([block, extra.astype(BF16)], axis=0)
            blocks.append(block)
        lhs = jnp.concatenate(blocks, axis=1)
        rhs = weights[row, pl.ds(col, 2)].reshape(2 * WIDTH, 2 * THREE)
        value = mm(lhs, rhs)

        @pl.when(i == 0)
        def _():
            total[...] = value

        @pl.when(i > 0)
        def _():
            total[...] += value

        return 0

    lax.fori_loop(first, last, body, 0)


def visible_pairs(documents):
    across = jnp.broadcast_to(documents, (ROWS, ROWS))
    down = across.T
    query = lax.broadcasted_iota(jnp.int32, (ROWS, ROWS), 0)
    key = lax.broadcasted_iota(jnp.int32, (ROWS, ROWS), 1)
    return (key <= query) & (across == down)


def probabilities(queries, keys, visible):
    scores = jnp.where(visible, mm(queries, keys, NT) * SCALE, -1e30)
    exponent = jnp.exp(scores - jnp.max(scores, -1, keepdims=True))
    return exponent / jnp.sum(exponent, -1, keepdims=True)


def kernel(
    x_prev, x_saved, g_next, w_qkv, w_out, gain, doc_ids,
    y_out, grad_out,
    sb, sg, sf, weights, w_o, gains, part_d, part_y,
    da1, da2, db1, db2, ya1, ya2, yb1, yb2,
    qkv_sum_b, qkv_sum_f, qkv_in, d_o, d_o_in, d_cat, o_cat,
    moments_held, moments_box, means_held, means_box,
    send_sems, recv_sems, local_sems,
):
    z, t = lax.axis_index("pipe"), lax.axis_index("tp")
    core, x, y = t % 2, (t // 2) % 4, t // 8
    planes = lax.axis_size("pipe")

    def at(dy, dx):
        return (z, (((y + dy) % 4) * 4 + (x + dx) % 4) * 2 + core)

    partner = (z, t + 1 - 2 * core)
    above, below = ((z + 1) % planes, t), ((z + planes - 1) % planes, t)
    near = {"xp": at(0, 1), "xm": at(0, 3), "yp": at(1, 0), "ym": at(3, 0)}
    x_far, y_far = at(0, 2), at(2, 0)

    barrier = pltpu.get_barrier_semaphore()
    everyone = [partner, above, below, x_far, y_far, *near.values()]
    for device in everyone:
        pl.semaphore_signal(barrier, inc=1, device_id=device, device_id_type=MESH)
    pl.semaphore_wait(barrier, len(everyone))

    wire = Wire(send_sems, recv_sems, partner)
    gb, gf, gg = (Gather(wire, near, slots) for slots in (sb, sf, sg))
    rd = Scatter(wire, near, part_d, da1, da2, db1, db2)
    ry = Scatter(wire, near, part_y, ya1, ya2, yb1, yb2)
    on_x, on_y = (near["xp"], near["xm"], x_far), (near["yp"], near["ym"], y_far)
    moments = AllSum(wire, partner, on_x, on_y, moments_held, moments_box)
    means = AllSum(wire, partner, on_x, on_y, means_held, means_box)
    swap_w, swap_o = wire.group(), wire.group()
    own_cols, their_cols = pl.ds(0, THREE), pl.ds(THREE, THREE)
    own_rows, their_rows = pl.ds(0, HEAD_DIM), pl.ds(HEAD_DIM, HEAD_DIM)

    gb.first(x_saved)
    shift_f = wire.send(x_prev, sf.at[0, 0], above)
    shift_g = wire.send(g_next, sg.at[0, 0], below)
    own_b = pltpu.make_async_copy(x_saved, sb.at[0, 0], local_sems.at[0])
    own_b.start()
    for py in range(4):
        for px in range(4):
            chip = ((y + OFFSET[py]) % 4) * 4 + (x + OFFSET[px]) % 4
            pltpu.make_async_copy(
                w_qkv.at[chip, core], weights.at[py, px, :, own_cols], local_sems.at[1]
            ).start()
            swap_w.send(w_qkv.at[chip, 1 - core], weights.at[py, px, :, their_cols], partner)
            pltpu.make_async_copy(
                gain.at[chip * 2 + core], gains.at[py, px], local_sems.at[3]
            ).start()
    own_b.wait()
    gb.second()
    for py in range(4):
        for px in range(4):
            chip = ((y + OFFSET[py]) % 4) * 4 + (x + OFFSET[px]) % 4
            mine = pl.multiple_of((chip * 2 + core) * WIDTH, 128)
            theirs = pl.multiple_of((chip * 2 + 1 - core) * WIDTH, 128)
            pltpu.make_async_copy(
                w_out.at[:, pl.ds(mine, WIDTH)], w_o.at[py, px, own_rows], local_sems.at[2]
            ).start()
            swap_o.send(w_out.at[:, pl.ds(theirs, WIDTH)], w_o.at[py, px, their_rows], partner)
    gb.third()
    shift_f.received()
    gf.first(sf.at[0, 0])
    moments.start(own_sums(sb[0, 0]) + own_sums(sf[0, 0]))
    gb.fourth()
    moments.along_x()
    gf.second()
    gb.fifth()
    moments.along_y()
    gf.third()
    shift_g.received()
    gg.first(sg.at[0, 0])
    total_b, square_b, total_f, square_f = moments.columns(4)
    center_b, inv_std_b = statistics(total_b, square_b)
    center_f, inv_std_f = statistics(total_f, square_f)

    gb.finish()
    pltpu.make_async_copy(gains, gains, local_sems.at[3]).wait()
    half_w = weights.at[:, :, :, own_cols]
    pltpu.make_async_copy(half_w, half_w, local_sems.at[1]).wait()
    swap_w.received(weights.at[:, :, :, their_cols])
    project(sb, gains, weights, qkv_sum_b, center_b, inv_std_b, True, 0, 3)
    gf.fourth()
    project(sb, gains, weights, qkv_sum_b, center_b, inv_std_b, True, 3, 6)
    gg.second()
    project(sb, gains, weights, qkv_sum_b, center_b, inv_std_b, True, 6, 8)
    trade_b = wire.send(qkv_sum_b.at[pl.ds(0, ROWS), their_cols], qkv_in.at[0], partner)
    gf.fifth()
    trade_b.received()
    qkv_b = qkv_sum_b[pl.ds(0, ROWS), own_cols] + qkv_in[0]
    low_b = qkv_b.astype(BF16)
    queries_b, keys_b, values_b = (low_b[:, k * HEAD_DIM : (k + 1) * HEAD_DIM] for k in range(3))
    probs_b = probabilities(queries_b, keys_b, visible_pairs(doc_ids[pl.ds(1, 1)]))
    gg.third()

    gf.finish()
    project(sf, gains, weights, qkv_sum_f, center_f, inv_std_f, False, 0, 8)
    trade_f = wire.send(qkv_sum_f.at[:, their_cols], qkv_in.at[1], partner)
    gg.fourth()
    gg.fifth()
    trade_f.received()
    low_f = (qkv_sum_f[:, own_cols] + qkv_in[1]).astype(BF16)
    queries, keys, values = (low_f[:, k * HEAD_DIM : (k + 1) * HEAD_DIM] for k in range(3))
    probs = probabilities(queries, keys, visible_pairs(doc_ids[pl.ds(0, 1)]))
    o_cat[:, own_rows] = mm(probs.astype(BF16), values).astype(BF16)
    trade_o = wire.send(o_cat.at[:, own_rows], o_cat.at[:, their_rows], partner)
    half_o = w_o.at[:, :, own_rows]
    pltpu.make_async_copy(half_o, half_o, local_sems.at[2]).wait()
    swap_o.received(w_o.at[:, :, their_rows])
    trade_o.received()
    o_all = o_cat[...]

    def output_blocks(py, px):
        rhs = jnp.concatenate([w_o[py, px], w_o[py, px + 1]], axis=1)
        value = mm(o_all, rhs).astype(BF16)
        part_y[py, px] = value[:, :WIDTH]
        part_y[py, px + 1] = value[:, WIDTH:]

    def scatter(reduction, blocks):
        blocks(3, 2)
        reduction.far(0, 0)
        reduction.far(0, 1)
        blocks(1, 2)
        blocks(2, 2)
        reduction.close(0, 0)
        reduction.far(1, 1)
        blocks(3, 0)
        reduction.close(0, 1)
        reduction.far(1, 0)
        blocks(0, 2)
        reduction.far(2, 0)
        reduction.far(2, 1)
        blocks(1, 0)
        blocks(2, 0)
        reduction.close(1, 0)
        reduction.close(1, 1)
        reduction.close(2, 0)
        blocks(0, 0)
        reduction.close(2, 1)

    scatter(ry, output_blocks)

    gg.finish()

    def output_gradient(i, total):
        row, col = i // 2, (i % 2) * 2
        lhs = jnp.concatenate([sg[row, col], sg[row, col + 1]], axis=1)
        rhs = jnp.concatenate([w_o[row, col], w_o[row, col + 1]], axis=1)
        return total + mm(lhs, rhs, NT)

    d_o[...] = lax.fori_loop(0, 8, output_gradient, jnp.zeros((ROWS, 2 * HEAD_DIM), F32))
    trade_d = wire.send(d_o.at[:, their_rows], d_o_in, partner)
    probs_low = probs_b.astype(BF16)
    ry.second(0)
    trade_d.received()
    d_low = (d_o[:, own_rows] + d_o_in[...]).astype(BF16)
    d_values = mm(probs_low, d_low, TN).astype(BF16)
    d_probs = mm(d_low, values_b, NT)
    d_scores = probs_b * (d_probs - jnp.sum(d_probs * probs_b, -1, keepdims=True)) * SCALE
    d_scores = d_scores.astype(BF16)
    d_queries = mm(d_scores, keys_b).astype(BF16)
    d_keys = mm(d_scores, queries_b, TN).astype(BF16)
    d_own = jnp.concatenate([d_queries, d_keys, d_values], axis=1)
    d_cat[:, own_cols] = d_own
    trade_c = wire.send(d_cat.at[:, own_cols], d_cat.at[:, their_cols], partner)
    ry.second(1)
    along_qkv = jnp.sum(d_own.astype(F32) * qkv_b, -1, keepdims=True)
    trade_c.received()

    d_all = d_cat[...]

    def input_blocks(py, px):
        rhs = weights[py, pl.ds(px, 2)].reshape(2 * WIDTH, 2 * THREE)
        value = mm(d_all, rhs, NT).astype(BF16)
        part_d[py, px] = value[:, :WIDTH]
        part_d[py, px + 1] = value[:, WIDTH:]

    scatter(rd, input_blocks)
    ry.second(2)

    gain_w = jnp.sum(qkv_sum_b[pl.ds(ROWS, 8)], 0, keepdims=True)
    along_gain = jnp.sum(d_all.astype(F32) * gain_w, -1, keepdims=True)
    means.start([along_gain, along_qkv])
    ry.third()
    rd.second(0)
    means.along_x()
    ry.fourth()
    rd.second(1)
    ry.fifth()
    means.along_y()
    rd.second(2)
    rd.third()
    y_out[...] = (sf[0, 0].astype(F32) + ry.finish()).astype(BF16)
    rd.fourth()
    mean_d, mean_dx = means.columns(2)
    x_hat = (sb[0, 0].astype(F32) - center_b) * inv_std_b
    rest = sg[0, 0].astype(F32) - inv_std_b * (mean_d + x_hat * mean_dx) * (1.0 / D)
    rd.fifth()
    all_sent = weights.at[:, 0, pl.ds(0, 240)]
    for one in (gb, gf, gg, ry):
        Group(one.sender, None, partner).sent(all_sent)
    for one in (
        shift_f, shift_g, trade_b, trade_f, trade_o, trade_d, trade_c, moments, means
    ):
        one.sent()
    swap_w.sent(weights.at[:, :, :, their_cols])
    swap_o.sent(w_o.at[:, :, their_rows])
    grad_out[...] = (rest + inv_std_b * (rd.finish() * gains[0, 0])).astype(BF16)
    Group(rd.sender, None, partner).sent(all_sent)


def place(y_ref, grad_ref, y_out, grad_out, sems):
    copies = [
        pltpu.make_async_copy(y_ref, y_out, sems.at[0]),
        pltpu.make_async_copy(grad_ref, grad_out, sems.at[1]),
    ]
    for copy in copies:
        copy.start()
    for copy in copies:
        copy.wait()


def shards(x_prev, x_saved, g_next, w_qkv, w_out, gain, doc_ids):
    block = (ROWS, WIDTH)
    grid = (4, 4)
    any_spec = pl.BlockSpec(memory_space=pl.ANY)
    vmem_spec = pl.BlockSpec(memory_space=pltpu.VMEM)
    scatter_space = [
        pltpu.VMEM((2, 2, 4, QUARTER, WIDTH), BF16),
        pltpu.VMEM((2, 2, 4, HALF, WIDTH), BF16),
        pltpu.VMEM((2, 2, QUARTER, WIDTH), BF16),
        pltpu.VMEM((2, 2, HALF, WIDTH), BF16),
    ]
    y_out, grad = pl.pallas_call(
        kernel,
        out_shape=[jax.ShapeDtypeStruct(block, BF16)] * 2,
        in_specs=[any_spec] * 6 + [vmem_spec],
        out_specs=[vmem_spec] * 2,
        scratch_shapes=[
            *[pltpu.VMEM(grid + block, BF16)] * 3,
            pltpu.VMEM(grid + (WIDTH, 2 * THREE), BF16),
            pltpu.VMEM(grid + (2 * HEAD_DIM, WIDTH), BF16),
            pltpu.VMEM(grid + (1, WIDTH), F32),
            *[pltpu.VMEM(grid + block, BF16)] * 2,
            *scatter_space,
            *scatter_space,
            pltpu.VMEM((ROWS + 16, 2 * THREE), F32),
            pltpu.VMEM((ROWS, 2 * THREE), F32),
            pltpu.VMEM((2, ROWS, THREE), F32),
            pltpu.VMEM((ROWS, 2 * HEAD_DIM), F32),
            pltpu.VMEM((ROWS, HEAD_DIM), F32),
            pltpu.VMEM((ROWS, 2 * THREE), BF16),
            pltpu.VMEM((ROWS, 2 * HEAD_DIM), BF16),
            *[pltpu.VMEM((3, 8, 128), F32), pltpu.VMEM((7, 8, 128), F32)] * 2,
            pltpu.SemaphoreType.DMA((N_SENDERS,)),
            pltpu.SemaphoreType.DMA((N_RECEIVERS,)),
            pltpu.SemaphoreType.DMA((4,)),
        ],
        compiler_params=pltpu.CompilerParams(
            collective_id=0, has_side_effects=True, vmem_limit_bytes=56 * 2**20
        ),
        name="section",
    )(
        x_prev[0],
        x_saved[0],
        g_next[0],
        w_qkv.reshape(16, 2, WIDTH, THREE),
        w_out[0],
        gain.reshape(32, 1, WIDTH),
        doc_ids[0],
    )
    y_out, grad = pl.pallas_call(
        place,
        out_shape=[jax.ShapeDtypeStruct(block, BF16)] * 2,
        in_specs=[vmem_spec] * 2,
        out_specs=[any_spec] * 2,
        scratch_shapes=[pltpu.SemaphoreType.DMA((2,))],
        name="place",
    )(y_out, grad)
    return y_out[None], grad[None]


def solution(mesh):
    in_specs = (
        P("pipe", None, "tp"),
        P("pipe", None, "tp"),
        P("pipe", None, "tp"),
        P("pipe", None, "tp", None),
        P("pipe", "tp", None),
        P("pipe", None),
        P("pipe", None, None),
    )
    out_specs = (P("pipe", None, "tp"), P("pipe", None, "tp"))
    return jax.shard_map(shards, mesh=mesh, in_specs=in_specs, out_specs=out_specs, check_vma=False)
```

```python
import functools
import math

import jax
import jax.numpy as jnp
from jax import lax
from jax.experimental import pallas as pl
from jax.experimental.pallas import tpu as pltpu
from jax.sharding import PartitionSpec as P

D = 12288
HEAD_DIM = 128
EPS = 1e-05
ROWS = 128
WIDTH = 384
HALF = 64
QUARTER = 32
THREE = 3 * HEAD_DIM
SCALE = 1.0 / math.sqrt(HEAD_DIM)
MESH = pl.DeviceIdType.MESH
F32 = jnp.float32
BF16 = jnp.bfloat16
NT = (((1,), (1,)), ((), ()))
TN = (((0,), (0,)), ((), ()))
N_SENDERS, N_RECEIVERS = 20, 46

OFFSET = (0, 1, 3, 2)


def mm(a, b, dims=None):
    if dims is None:
        return jnp.dot(a, b, preferred_element_type=F32)
    return lax.dot_general(a, b, dims, preferred_element_type=F32)


class Wire:
    def __init__(self, send_sems, recv_sems, partner):
        self.send_sems, self.recv_sems, self.partner = send_sems, recv_sems, partner
        self.sends = self.receives = 0

    def sender(self):
        self.sends += 1
        return self.send_sems.at[self.sends - 1]

    def group(self, send_sem=None):
        self.receives += 1
        receiver = self.recv_sems.at[self.receives - 1]
        return Group(self.sender() if send_sem is None else send_sem, receiver, self.partner)

    def send(self, src, dst, device):
        group = self.group()
        group.send(src, dst, device)
        return group


class Group:
    def __init__(self, send_sem, recv_sem, partner):
        self.send_sem, self.recv_sem, self.partner = send_sem, recv_sem, partner

    def _copy(self, src, dst, device):
        return pltpu.make_async_remote_copy(
            src_ref=src,
            dst_ref=dst,
            send_sem=self.send_sem,
            recv_sem=self.recv_sem,
            device_id=device,
            device_id_type=MESH,
        )

    def send(self, src, dst, device):
        self.last = self._copy(src, dst, device)
        self.last.start()

    def received(self, like=None):
        (self.last if like is None else self._copy(like, like, self.partner)).wait_recv()

    def sent(self, like=None):
        (self.last if like is None else self._copy(like, like, self.partner)).wait_send()


class Gather:
    def __init__(self, wire, near, slots):
        self.near, self.slots = near, slots
        self.sender = wire.sender()
        self.one, self.two, self.three, self.more, self.four = (
            wire.group(self.sender) for _ in range(5)
        )

    def first(self, own):
        s, n, g = self.slots, self.near, self.one
        a, b = pl.ds(0, HALF), pl.ds(HALF, HALF)
        g.send(own.at[a], s.at[0, 2, a], n["xp"])
        g.send(own.at[b], s.at[2, 0, b], n["yp"])
        g.send(own.at[a], s.at[0, 1, a], n["xm"])
        g.send(own.at[b], s.at[1, 0, b], n["ym"])

    def second(self):
        s, n, g = self.slots, self.near, self.two
        self.one.received(s.at[0, pl.ds(0, 2)])
        a0, a1 = pl.ds(0, QUARTER), pl.ds(QUARTER, QUARTER)
        b0, b1 = pl.ds(HALF, QUARTER), pl.ds(HALF + QUARTER, QUARTER)
        g.send(s.at[0, 2, a0], s.at[0, 3, a0], n["xp"])
        g.send(s.at[2, 0, b0], s.at[3, 0, b0], n["yp"])
        g.send(s.at[0, 1, a1], s.at[0, 3, a1], n["xm"])
        g.send(s.at[1, 0, b1], s.at[3, 0, b1], n["ym"])
        self._across(self.three, pl.ds(0, 3))

    def third(self):
        self.two.received(self.slots.at[0, 0])
        self._across(self.more, pl.ds(3, 1))

    def _across(self, g, part):
        s, n = self.slots, self.near
        a, b = pl.ds(0, HALF), pl.ds(HALF, HALF)
        g.send(s.at[0, part, a], s.at[2, part, a], n["yp"])
        g.send(s.at[part, 0, b], s.at[part, 2, b], n["xp"])
        g.send(s.at[0, part, a], s.at[1, part, a], n["ym"])
        g.send(s.at[part, 0, b], s.at[part, 1, b], n["xm"])

    def _onward(self, part):
        s, n, g = self.slots, self.near, self.four
        a0, a1 = pl.ds(0, QUARTER), pl.ds(QUARTER, QUARTER)
        b0, b1 = pl.ds(HALF, QUARTER), pl.ds(HALF + QUARTER, QUARTER)
        g.send(s.at[2, part, a0], s.at[3, part, a0], n["yp"])
        g.send(s.at[part, 2, b0], s.at[part, 3, b0], n["xp"])
        g.send(s.at[1, part, a1], s.at[3, part, a1], n["ym"])
        g.send(s.at[part, 1, b1], s.at[part, 3, b1], n["xm"])

    def fourth(self):
        self.three.received(self.slots.at[pl.ds(0, 3), pl.ds(0, 2)])
        self._onward(pl.ds(0, 3))

    def fifth(self):
        self.more.received(self.slots.at[0, pl.ds(0, 2)])
        self._onward(pl.ds(3, 1))

    def finish(self):
        self.four.received(self.slots.at[0])


def add_into(target, *terms):
    total = target[...].astype(F32)
    for term in terms:
        total = total + term[...].astype(F32)
    target[...] = total.astype(BF16)


PIECES = ((3, 1), (1, 2), (0, 1))


class Scatter:
    def __init__(self, wire, near, parts, a1, a2, b1, b2):
        self.near, self.parts = near, parts
        self.a1, self.a2, self.b1, self.b2 = a1, a2, b1, b2
        self.sender = wire.sender()
        self.one = [wire.group(self.sender) for _ in range(4)]
        self.two = [wire.group(self.sender) for _ in range(4)]

    def _part(self, half, pos, rows, k):
        rows = pl.ds(half * HALF + rows, QUARTER)
        if k < 3:
            first, second = pos, pl.ds(*PIECES[k])
        else:
            first, second = 0, pos
        return self.parts.at[(first, second, rows) if half == 0 else (second, first, rows)]

    def _box(self, half, way, rows, k):
        rows = pl.ds(rows, QUARTER)
        if k < 3:
            piece = pl.ds(*PIECES[k])
            return self.a1.at[half, way, piece], self.a2.at[half, way, piece, rows]
        return self.b1.at[half, way], self.b2.at[half, way, rows]

    def _ways(self, half, k):
        axis = "y" if (half == 0) == (k < 3) else "x"
        return self.near[axis + "p"], self.near[axis + "m"]

    def far(self, k, half):
        for way, device in enumerate(self._ways(half, k)):
            self.one[k].send(
                self._part(half, 3, way * QUARTER, k), self._box(half, way, 0, k)[0], device
            )

    def close(self, k, half):
        for way, device in enumerate(self._ways(half, k)):
            rows = (1 - way) * QUARTER
            self.two[k].send(
                self._part(half, 1 + way, rows, k), self._box(half, way, rows, k)[1], device
            )

    def _pass(self, k):
        for half in (0, 1):
            for way, device in enumerate(self._ways(half, k)):
                part = self._part(half, 1 + way, way * QUARTER, k)
                add_into(part, self._box(half, way, 0, k)[0])
                self.two[k].send(part, self._box(half, way, way * QUARTER, k)[1], device)

    def _fold(self, half, pos):
        for q in (0, QUARTER):
            rows = pl.ds(q, QUARTER)
            add_into(
                self._part(half, pos, q, 3),
                self.a2.at[half, 0, pos, rows],
                self.a2.at[half, 1, pos, rows],
            )

    def second(self, k):
        self.one[k].received(self.parts.at[0, pl.ds(0, PIECES[k][1])])
        self._pass(k)

    def third(self):
        self.two[0].received(self.parts.at[0, pl.ds(0, 2)])
        for half in (0, 1):
            self._fold(half, 3)
            self.far(3, half)

    def fourth(self):
        self.two[1].received(self.parts.at[0])
        for half in (0, 1):
            self._fold(half, 1)
            self._fold(half, 2)
            self.close(3, half)

    def fifth(self):
        self.one[3].received(self.parts.at[0, 0])
        self._pass(3)

    def finish(self):
        self.two[2].received(self.parts.at[0, pl.ds(0, 2)])
        self.two[3].received(self.parts.at[0, pl.ds(0, 2)])
        halves = []
        for half in (0, 1):
            total = self.parts[0, 0, pl.ds(half * HALF, HALF)].astype(F32)
            for term in (
                self.a2[half, 0, 0], self.a2[half, 1, 0], self.b2[half, 0], self.b2[half, 1]
            ):
                total = total + term.astype(F32)
            halves.append(total)
        return jnp.concatenate(halves, axis=0)


class AllSum:
    def __init__(self, wire, partner, along_x, along_y, held, box):
        self.held, self.box, self.partner, self.x, self.y = held, box, partner, along_x, along_y
        self.groups = [wire.group() for _ in range(3)]

    def start(self, columns):
        lane = lax.broadcasted_iota(jnp.int32, (ROWS, 128), 1)
        square = jnp.zeros((ROWS, 128), F32)
        for k, column in enumerate(columns):
            square = jnp.where(lane == k, column, square)
        self.held[0] = square.T[:8]
        self.groups[0].send(self.held.at[0], self.box.at[0], self.partner)

    def along_x(self):
        self.groups[0].received()
        self.held[1] = self.held[0] + self.box[0]
        for k, device in enumerate(self.x):
            self.groups[1].send(self.held.at[1], self.box.at[1 + k], device)

    def along_y(self):
        self.groups[1].received(self.box.at[pl.ds(1, 3)])
        self.held[2] = self.held[1] + self.box[1] + self.box[2] + self.box[3]
        for k, device in enumerate(self.y):
            self.groups[2].send(self.held.at[2], self.box.at[4 + k], device)

    def columns(self, count):
        self.groups[2].received(self.box.at[pl.ds(4, 3)])
        total = self.held[2] + self.box[4] + self.box[5] + self.box[6]
        square = jnp.concatenate([total, jnp.zeros((ROWS - 8, 128), F32)], axis=0).T
        return [square[:, k : k + 1] for k in range(count)]

    def sent(self):
        self.groups[0].sent()
        self.groups[1].sent(self.box.at[pl.ds(1, 3)])
        self.groups[2].sent(self.box.at[pl.ds(4, 3)])


def own_sums(block):
    values = block.astype(F32)
    return [jnp.sum(v, -1, keepdims=True) for v in (values, values * values)]


def statistics(total, square):
    center = total * (1.0 / D)
    return center, lax.rsqrt(square * (1.0 / D) - center * center + EPS)


def project(slots, gains, weights, total, center, inv_std, with_gain, first, last):
    def body(i, _):
        row, col = i % 4, (i // 4) * 2
        blocks = []
        for k in range(2):
            gain = gains[row, col + k]
            hidden = (slots[row, col + k].astype(F32) - center) * inv_std * gain
            block = hidden.astype(BF16)
            if with_gain:
                high = gain.astype(BF16).astype(F32)
                middle = (gain - high).astype(BF16).astype(F32)
                low = gain - high - middle
                at = lax.broadcasted_iota(jnp.int32, (16, WIDTH), 0)
                extra = jnp.where(at == 0, high, jnp.where(at == 1, middle, low))
                extra = jnp.where(at < 3, extra, 0.0)
                block = jnp.concatenate([block, extra.astype(BF16)], axis=0)
            blocks.append(block)
        lhs = jnp.concatenate(blocks, axis=1)
        rhs = weights[row, pl.ds(col, 2)].reshape(2 * WIDTH, 2 * THREE)
        value = mm(lhs, rhs)

        @pl.when(i == 0)
        def _():
            total[...] = value

        @pl.when(i > 0)
        def _():
            total[...] += value

        return 0

    lax.fori_loop(first, last, body, 0)


def visible_pairs(documents):
    across = jnp.broadcast_to(documents, (ROWS, ROWS))
    down = across.T
    query = lax.broadcasted_iota(jnp.int32, (ROWS, ROWS), 0)
    key = lax.broadcasted_iota(jnp.int32, (ROWS, ROWS), 1)
    return (key <= query) & (across == down)


def probabilities(queries, keys, visible):
    scores = jnp.where(visible, mm(queries, keys, NT) * SCALE, -1e30)
    exponent = jnp.exp(scores - jnp.max(scores, -1, keepdims=True))
    return exponent / jnp.sum(exponent, -1, keepdims=True)


def kernel(
    x_prev, x_saved, g_next, w_qkv, w_out, gain, documents,
    y_out, grad_out,
    sb, sg, sf, weights, w_o, gains, part_d, part_y,
    da1, da2, db1, db2, ya1, ya2, yb1, yb2,
    qkv_sum_b, qkv_sum_f, qkv_in, d_o, d_o_in, d_cat, o_cat,
    moments_held, moments_box, means_held, means_box, doc_ids,
    send_sems, recv_sems, local_sems,
):
    z, t = lax.axis_index("pipe"), lax.axis_index("tp")
    core, x, y = t % 2, (t // 2) % 4, t // 8
    planes = lax.axis_size("pipe")

    def at(dy, dx):
        return (z, (((y + dy) % 4) * 4 + (x + dx) % 4) * 2 + core)

    partner = (z, t + 1 - 2 * core)
    above, below = ((z + 1) % planes, t), ((z + planes - 1) % planes, t)
    near = {"xp": at(0, 1), "xm": at(0, 3), "yp": at(1, 0), "ym": at(3, 0)}
    x_far, y_far = at(0, 2), at(2, 0)

    barrier = pltpu.get_barrier_semaphore()
    everyone = [partner, above, below, x_far, y_far, *near.values()]
    for device in everyone:
        pl.semaphore_signal(barrier, inc=1, device_id=device, device_id_type=MESH)
    pl.semaphore_wait(barrier, len(everyone))

    wire = Wire(send_sems, recv_sems, partner)
    gb, gf, gg = (Gather(wire, near, slots) for slots in (sb, sf, sg))
    rd = Scatter(wire, near, part_d, da1, da2, db1, db2)
    ry = Scatter(wire, near, part_y, ya1, ya2, yb1, yb2)
    on_x, on_y = (near["xp"], near["xm"], x_far), (near["yp"], near["ym"], y_far)
    moments = AllSum(wire, partner, on_x, on_y, moments_held, moments_box)
    means = AllSum(wire, partner, on_x, on_y, means_held, means_box)
    swap_w, swap_o = wire.group(), wire.group()
    own_cols, their_cols = pl.ds(0, THREE), pl.ds(THREE, THREE)
    own_rows, their_rows = pl.ds(0, HEAD_DIM), pl.ds(HEAD_DIM, HEAD_DIM)

    gb.first(x_saved)
    shift_f = wire.send(x_prev, sf.at[0, 0], above)
    shift_g = wire.send(g_next, sg.at[0, 0], below)
    own_b = pltpu.make_async_copy(x_saved, sb.at[0, 0], local_sems.at[0])
    own_b.start()
    for py in range(4):
        for px in range(4):
            chip = ((y + OFFSET[py]) % 4) * 4 + (x + OFFSET[px]) % 4
            pltpu.make_async_copy(
                w_qkv.at[chip, core], weights.at[py, px, :, own_cols], local_sems.at[1]
            ).start()
            swap_w.send(w_qkv.at[chip, 1 - core], weights.at[py, px, :, their_cols], partner)
            pltpu.make_async_copy(
                gain.at[chip * 2 + core], gains.at[py, px], local_sems.at[3]
            ).start()
    own_docs = pltpu.make_async_copy(documents, doc_ids, local_sems.at[4])
    own_docs.start()
    own_b.wait()
    gb.second()
    for py in range(4):
        for px in range(4):
            chip = ((y + OFFSET[py]) % 4) * 4 + (x + OFFSET[px]) % 4
            mine = pl.multiple_of((chip * 2 + core) * WIDTH, 128)
            theirs = pl.multiple_of((chip * 2 + 1 - core) * WIDTH, 128)
            pltpu.make_async_copy(
                w_out.at[:, pl.ds(mine, WIDTH)], w_o.at[py, px, own_rows], local_sems.at[2]
            ).start()
            swap_o.send(w_out.at[:, pl.ds(theirs, WIDTH)], w_o.at[py, px, their_rows], partner)
    gb.third()
    shift_f.received()
    gf.first(sf.at[0, 0])
    moments.start(own_sums(sb[0, 0]) + own_sums(sf[0, 0]))
    gb.fourth()
    moments.along_x()
    gf.second()
    gb.fifth()
    moments.along_y()
    gf.third()
    shift_g.received()
    gg.first(sg.at[0, 0])
    total_b, square_b, total_f, square_f = moments.columns(4)
    center_b, inv_std_b = statistics(total_b, square_b)
    center_f, inv_std_f = statistics(total_f, square_f)

    pltpu.make_async_copy(gains, gains, local_sems.at[3]).wait()
    half_w = weights.at[:, :, :, own_cols]
    pltpu.make_async_copy(half_w, half_w, local_sems.at[1]).wait()
    swap_w.received(weights.at[:, :, :, their_cols])
    own_docs.wait()

    def project_b(first, last):
        project(sb, gains, weights, qkv_sum_b, center_b, inv_std_b, True, first, last)

    def project_f(first, last):
        project(sf, gains, weights, qkv_sum_f, center_f, inv_std_f, False, first, last)

    project_b(0, 3)
    gb.finish()
    project_b(3, 6)
    gf.fourth()
    gf.fifth()
    gg.second()
    project_b(6, 8)
    trade_b = wire.send(qkv_sum_b.at[pl.ds(0, ROWS), their_cols], qkv_in.at[0], partner)
    project_f(0, 3)
    gg.third()
    gf.finish()
    project_f(3, 8)
    trade_f = wire.send(qkv_sum_f.at[:, their_cols], qkv_in.at[1], partner)

    trade_b.received()
    qkv_b = qkv_sum_b[pl.ds(0, ROWS), own_cols] + qkv_in[0]
    low_b = qkv_b.astype(BF16)
    queries_b, keys_b, values_b = (low_b[:, k * HEAD_DIM : (k + 1) * HEAD_DIM] for k in range(3))
    probs_b = probabilities(queries_b, keys_b, visible_pairs(doc_ids[pl.ds(1, 1)]))
    gg.fourth()

    trade_f.received()
    low_f = (qkv_sum_f[:, own_cols] + qkv_in[1]).astype(BF16)
    queries, keys, values = (low_f[:, k * HEAD_DIM : (k + 1) * HEAD_DIM] for k in range(3))
    probs = probabilities(queries, keys, visible_pairs(doc_ids[pl.ds(0, 1)]))
    o_cat[:, own_rows] = mm(probs.astype(BF16), values).astype(BF16)
    trade_o = wire.send(o_cat.at[:, own_rows], o_cat.at[:, their_rows], partner)
    gg.fifth()
    half_o = w_o.at[:, :, own_rows]
    pltpu.make_async_copy(half_o, half_o, local_sems.at[2]).wait()
    swap_o.received(w_o.at[:, :, their_rows])

    def output_gradient(i, total):
        row, col = i % 4, (i // 4) * 2
        lhs = jnp.concatenate([sg[row, col], sg[row, col + 1]], axis=1)
        rhs = jnp.concatenate([w_o[row, col], w_o[row, col + 1]], axis=1)
        return total + mm(lhs, rhs, NT)

    d_o[...] = lax.fori_loop(0, 3, output_gradient, jnp.zeros((ROWS, 2 * HEAD_DIM), F32))
    trade_o.received()
    o_all = o_cat[...]

    def output_blocks(py, px):
        rhs = jnp.concatenate([w_o[py, px], w_o[py, px + 1]], axis=1)
        value = mm(o_all, rhs).astype(BF16)
        part_y[py, px] = value[:, :WIDTH]
        part_y[py, px + 1] = value[:, WIDTH:]

    def scatter(reduction, blocks):
        blocks(3, 2)
        reduction.far(0, 0)
        reduction.far(0, 1)
        blocks(1, 2)
        blocks(2, 2)
        reduction.close(0, 0)
        reduction.far(1, 1)
        blocks(3, 0)
        reduction.close(0, 1)
        reduction.far(1, 0)
        blocks(0, 2)
        reduction.far(2, 0)
        reduction.far(2, 1)
        blocks(1, 0)
        blocks(2, 0)
        reduction.close(1, 0)
        reduction.close(1, 1)
        reduction.close(2, 0)
        blocks(0, 0)
        reduction.close(2, 1)

    scatter(ry, output_blocks)

    gg.finish()

    d_o[...] = lax.fori_loop(3, 8, output_gradient, d_o[...])
    trade_d = wire.send(d_o.at[:, their_rows], d_o_in, partner)
    probs_low = probs_b.astype(BF16)
    ry.second(0)
    trade_d.received()
    d_low = (d_o[:, own_rows] + d_o_in[...]).astype(BF16)
    d_values = mm(probs_low, d_low, TN).astype(BF16)
    d_probs = mm(d_low, values_b, NT)
    d_scores = probs_b * (d_probs - jnp.sum(d_probs * probs_b, -1, keepdims=True)) * SCALE
    d_scores = d_scores.astype(BF16)
    d_queries = mm(d_scores, keys_b).astype(BF16)
    d_keys = mm(d_scores, queries_b, TN).astype(BF16)
    d_own = jnp.concatenate([d_queries, d_keys, d_values], axis=1)
    d_cat[:, own_cols] = d_own
    trade_c = wire.send(d_cat.at[:, own_cols], d_cat.at[:, their_cols], partner)
    ry.second(1)
    along_qkv = jnp.sum(d_own.astype(F32) * qkv_b, -1, keepdims=True)
    trade_c.received()

    d_all = d_cat[...]

    def input_blocks(py, px):
        rhs = weights[py, pl.ds(px, 2)].reshape(2 * WIDTH, 2 * THREE)
        value = mm(d_all, rhs, NT).astype(BF16)
        part_d[py, px] = value[:, :WIDTH]
        part_d[py, px + 1] = value[:, WIDTH:]

    scatter(rd, input_blocks)
    ry.second(2)

    gain_w = jnp.sum(qkv_sum_b[pl.ds(ROWS, 8)], 0, keepdims=True)
    along_gain = jnp.sum(d_all.astype(F32) * gain_w, -1, keepdims=True)
    means.start([along_gain, along_qkv])
    ry.third()
    rd.second(0)
    means.along_x()
    ry.fourth()
    rd.second(1)
    ry.fifth()
    means.along_y()
    rd.second(2)
    rd.third()
    y_out[...] = (sf[0, 0].astype(F32) + ry.finish()).astype(BF16)
    rd.fourth()
    mean_d, mean_dx = means.columns(2)
    x_hat = (sb[0, 0].astype(F32) - center_b) * inv_std_b
    rest = sg[0, 0].astype(F32) - inv_std_b * (mean_d + x_hat * mean_dx) * (1.0 / D)
    rd.fifth()
    all_sent = weights.at[:, 0, pl.ds(0, 240)]
    for one in (gb, gf, gg, ry):
        Group(one.sender, None, partner).sent(all_sent)
    for one in (
        shift_f, shift_g, trade_b, trade_f, trade_o, trade_d, trade_c, moments, means
    ):
        one.sent()
    swap_w.sent(weights.at[:, :, :, their_cols])
    swap_o.sent(w_o.at[:, :, their_rows])
    grad_out[...] = (rest + inv_std_b * (rd.finish() * gains[0, 0])).astype(BF16)
    Group(rd.sender, None, partner).sent(all_sent)


def place(y_ref, grad_ref, y_out, grad_out, sems):
    copies = [
        pltpu.make_async_copy(y_ref, y_out, sems.at[0]),
        pltpu.make_async_copy(grad_ref, grad_out, sems.at[1]),
    ]
    for copy in copies:
        copy.start()
    for copy in copies:
        copy.wait()


def shards(x_prev, x_saved, g_next, w_qkv, w_out, gain, doc_ids):
    block = (ROWS, WIDTH)
    grid = (4, 4)
    any_spec = pl.BlockSpec(memory_space=pl.ANY)
    vmem_spec = pl.BlockSpec(memory_space=pltpu.VMEM)
    scatter_space = [
        pltpu.VMEM((2, 2, 4, QUARTER, WIDTH), BF16),
        pltpu.VMEM((2, 2, 4, HALF, WIDTH), BF16),
        pltpu.VMEM((2, 2, QUARTER, WIDTH), BF16),
        pltpu.VMEM((2, 2, HALF, WIDTH), BF16),
    ]
    y_out, grad = pl.pallas_call(
        kernel,
        out_shape=[jax.ShapeDtypeStruct(block, BF16)] * 2,
        in_specs=[any_spec] * 7,
        out_specs=[vmem_spec] * 2,
        scratch_shapes=[
            *[pltpu.VMEM(grid + block, BF16)] * 3,
            pltpu.VMEM(grid + (WIDTH, 2 * THREE), BF16),
            pltpu.VMEM(grid + (2 * HEAD_DIM, WIDTH), BF16),
            pltpu.VMEM(grid + (1, WIDTH), F32),
            *[pltpu.VMEM(grid + block, BF16)] * 2,
            *scatter_space,
            *scatter_space,
            pltpu.VMEM((ROWS + 16, 2 * THREE), F32),
            pltpu.VMEM((ROWS, 2 * THREE), F32),
            pltpu.VMEM((2, ROWS, THREE), F32),
            pltpu.VMEM((ROWS, 2 * HEAD_DIM), F32),
            pltpu.VMEM((ROWS, HEAD_DIM), F32),
            pltpu.VMEM((ROWS, 2 * THREE), BF16),
            pltpu.VMEM((ROWS, 2 * HEAD_DIM), BF16),
            *[pltpu.VMEM((3, 8, 128), F32), pltpu.VMEM((7, 8, 128), F32)] * 2,
            pltpu.VMEM((2, ROWS), jnp.int32),
            pltpu.SemaphoreType.DMA((N_SENDERS,)),
            pltpu.SemaphoreType.DMA((N_RECEIVERS,)),
            pltpu.SemaphoreType.DMA((5,)),
        ],
        compiler_params=pltpu.CompilerParams(
            collective_id=0, has_side_effects=True, vmem_limit_bytes=56 * 2**20
        ),
        name="section",
    )(
        x_prev[0],
        x_saved[0],
        g_next[0],
        w_qkv.reshape(16, 2, WIDTH, THREE),
        w_out[0],
        gain.reshape(32, 1, WIDTH),
        doc_ids[0],
    )
    y_out, grad = pl.pallas_call(
        place,
        out_shape=[jax.ShapeDtypeStruct(block, BF16)] * 2,
        in_specs=[vmem_spec] * 2,
        out_specs=[any_spec] * 2,
        scratch_shapes=[pltpu.SemaphoreType.DMA((2,))],
        name="place",
    )(y_out, grad)
    return y_out[None], grad[None]


def solution(mesh):
    in_specs = (
        P("pipe", None, "tp"),
        P("pipe", None, "tp"),
        P("pipe", None, "tp"),
        P("pipe", None, "tp", None),
        P("pipe", "tp", None),
        P("pipe", None),
        P("pipe", None, None),
    )
    out_specs = (P("pipe", None, "tp"), P("pipe", None, "tp"))
    return jax.shard_map(shards, mesh=mesh, in_specs=in_specs, out_specs=out_specs, check_vma=False)
```

```python
import functools
import math

import jax
import jax.numpy as jnp
from jax import lax
from jax.experimental import pallas as pl
from jax.experimental.pallas import tpu as pltpu
from jax.sharding import PartitionSpec as P

D = 12288
HEAD_DIM = 128
EPS = 1e-05
ROWS = 128
WIDTH = 384
HALF = 64
QUARTER = 32
THREE = 3 * HEAD_DIM
SCALE = 1.0 / math.sqrt(HEAD_DIM)
MESH = pl.DeviceIdType.MESH
F32 = jnp.float32
BF16 = jnp.bfloat16
NT = (((1,), (1,)), ((), ()))
TN = (((0,), (0,)), ((), ()))
N_SENDERS, N_RECEIVERS = 20, 46

OFFSET = (0, 1, 3, 2)


def mm(a, b, dims=None):
    if dims is None:
        return jnp.dot(a, b, preferred_element_type=F32)
    return lax.dot_general(a, b, dims, preferred_element_type=F32)


class Wire:
    def __init__(self, send_sems, recv_sems, partner):
        self.send_sems, self.recv_sems, self.partner = send_sems, recv_sems, partner
        self.sends = self.receives = 0

    def sender(self):
        self.sends += 1
        return self.send_sems.at[self.sends - 1]

    def group(self, send_sem=None):
        self.receives += 1
        receiver = self.recv_sems.at[self.receives - 1]
        return Group(self.sender() if send_sem is None else send_sem, receiver, self.partner)

    def send(self, src, dst, device):
        group = self.group()
        group.send(src, dst, device)
        return group


class Group:
    def __init__(self, send_sem, recv_sem, partner):
        self.send_sem, self.recv_sem, self.partner = send_sem, recv_sem, partner

    def _copy(self, src, dst, device):
        return pltpu.make_async_remote_copy(
            src_ref=src,
            dst_ref=dst,
            send_sem=self.send_sem,
            recv_sem=self.recv_sem,
            device_id=device,
            device_id_type=MESH,
        )

    def send(self, src, dst, device):
        self.last = self._copy(src, dst, device)
        self.last.start()

    def received(self, like=None):
        (self.last if like is None else self._copy(like, like, self.partner)).wait_recv()

    def sent(self, like=None):
        (self.last if like is None else self._copy(like, like, self.partner)).wait_send()


class Gather:
    def __init__(self, wire, near, slots):
        self.near, self.slots = near, slots
        self.sender = wire.sender()
        self.one, self.two, self.three, self.more, self.four = (
            wire.group(self.sender) for _ in range(5)
        )

    def first(self, own):
        s, n, g = self.slots, self.near, self.one
        a, b = pl.ds(0, HALF), pl.ds(HALF, HALF)
        g.send(own.at[a], s.at[0, 2, a], n["xp"])
        g.send(own.at[b], s.at[2, 0, b], n["yp"])
        g.send(own.at[a], s.at[0, 1, a], n["xm"])
        g.send(own.at[b], s.at[1, 0, b], n["ym"])

    def second(self):
        s, n, g = self.slots, self.near, self.two
        self.one.received(s.at[0, pl.ds(0, 2)])
        a0, a1 = pl.ds(0, QUARTER), pl.ds(QUARTER, QUARTER)
        b0, b1 = pl.ds(HALF, QUARTER), pl.ds(HALF + QUARTER, QUARTER)
        g.send(s.at[0, 2, a0], s.at[0, 3, a0], n["xp"])
        g.send(s.at[2, 0, b0], s.at[3, 0, b0], n["yp"])
        g.send(s.at[0, 1, a1], s.at[0, 3, a1], n["xm"])
        g.send(s.at[1, 0, b1], s.at[3, 0, b1], n["ym"])
        self._across(self.three, pl.ds(0, 3))

    def third(self):
        self.two.received(self.slots.at[0, 0])
        self._across(self.more, pl.ds(3, 1))

    def _across(self, g, part):
        s, n = self.slots, self.near
        a, b = pl.ds(0, HALF), pl.ds(HALF, HALF)
        g.send(s.at[0, part, a], s.at[2, part, a], n["yp"])
        g.send(s.at[part, 0, b], s.at[part, 2, b], n["xp"])
        g.send(s.at[0, part, a], s.at[1, part, a], n["ym"])
        g.send(s.at[part, 0, b], s.at[part, 1, b], n["xm"])

    def _onward(self, part):
        s, n, g = self.slots, self.near, self.four
        a0, a1 = pl.ds(0, QUARTER), pl.ds(QUARTER, QUARTER)
        b0, b1 = pl.ds(HALF, QUARTER), pl.ds(HALF + QUARTER, QUARTER)
        g.send(s.at[2, part, a0], s.at[3, part, a0], n["yp"])
        g.send(s.at[part, 2, b0], s.at[part, 3, b0], n["xp"])
        g.send(s.at[1, part, a1], s.at[3, part, a1], n["ym"])
        g.send(s.at[part, 1, b1], s.at[part, 3, b1], n["xm"])

    def fourth(self):
        self.three.received(self.slots.at[pl.ds(0, 3), pl.ds(0, 2)])
        self._onward(pl.ds(0, 3))

    def fifth(self):
        self.more.received(self.slots.at[0, pl.ds(0, 2)])
        self._onward(pl.ds(3, 1))

    def finish(self):
        self.four.received(self.slots.at[0])


def add_into(target, *terms):
    total = target[...].astype(F32)
    for term in terms:
        total = total + term[...].astype(F32)
    target[...] = total.astype(BF16)


PIECES = ((3, 1), (1, 2), (0, 1))


class Scatter:
    def __init__(self, wire, near, parts, a1, a2, b1, b2):
        self.near, self.parts = near, parts
        self.a1, self.a2, self.b1, self.b2 = a1, a2, b1, b2
        self.sender = wire.sender()
        self.one = [wire.group(self.sender) for _ in range(4)]
        self.two = [wire.group(self.sender) for _ in range(4)]

    def _part(self, half, pos, rows, k):
        rows = pl.ds(half * HALF + rows, QUARTER)
        if k < 3:
            first, second = pos, pl.ds(*PIECES[k])
        else:
            first, second = 0, pos
        return self.parts.at[(first, second, rows) if half == 0 else (second, first, rows)]

    def _box(self, half, way, rows, k):
        rows = pl.ds(rows, QUARTER)
        if k < 3:
            piece = pl.ds(*PIECES[k])
            return self.a1.at[half, way, piece], self.a2.at[half, way, piece, rows]
        return self.b1.at[half, way], self.b2.at[half, way, rows]

    def _ways(self, half, k):
        axis = "y" if (half == 0) == (k < 3) else "x"
        return self.near[axis + "p"], self.near[axis + "m"]

    def far(self, k, half):
        for way, device in enumerate(self._ways(half, k)):
            self.one[k].send(
                self._part(half, 3, way * QUARTER, k), self._box(half, way, 0, k)[0], device
            )

    def close(self, k, half):
        for way, device in enumerate(self._ways(half, k)):
            rows = (1 - way) * QUARTER
            self.two[k].send(
                self._part(half, 1 + way, rows, k), self._box(half, way, rows, k)[1], device
            )

    def _pass(self, k):
        for half in (0, 1):
            for way, device in enumerate(self._ways(half, k)):
                part = self._part(half, 1 + way, way * QUARTER, k)
                add_into(part, self._box(half, way, 0, k)[0])
                self.two[k].send(part, self._box(half, way, way * QUARTER, k)[1], device)

    def _fold(self, half, pos):
        for q in (0, QUARTER):
            rows = pl.ds(q, QUARTER)
            add_into(
                self._part(half, pos, q, 3),
                self.a2.at[half, 0, pos, rows],
                self.a2.at[half, 1, pos, rows],
            )

    def second(self, k):
        self.one[k].received(self.parts.at[0, pl.ds(0, PIECES[k][1])])
        self._pass(k)

    def third(self):
        self.two[0].received(self.parts.at[0, pl.ds(0, 2)])
        for half in (0, 1):
            self._fold(half, 3)
            self.far(3, half)

    def fourth(self):
        self.two[1].received(self.parts.at[0])
        for half in (0, 1):
            self._fold(half, 1)
            self._fold(half, 2)
            self.close(3, half)

    def fifth(self):
        self.one[3].received(self.parts.at[0, 0])
        self._pass(3)

    def finish(self):
        self.two[2].received(self.parts.at[0, pl.ds(0, 2)])
        self.two[3].received(self.parts.at[0, pl.ds(0, 2)])
        halves = []
        for half in (0, 1):
            total = self.parts[0, 0, pl.ds(half * HALF, HALF)].astype(F32)
            for term in (
                self.a2[half, 0, 0], self.a2[half, 1, 0], self.b2[half, 0], self.b2[half, 1]
            ):
                total = total + term.astype(F32)
            halves.append(total)
        return jnp.concatenate(halves, axis=0)


class AllSum:
    def __init__(self, wire, partner, along_x, along_y, held, box):
        self.held, self.box, self.partner, self.x, self.y = held, box, partner, along_x, along_y
        self.groups = [wire.group() for _ in range(3)]

    def start(self, columns):
        lane = lax.broadcasted_iota(jnp.int32, (ROWS, 128), 1)
        square = jnp.zeros((ROWS, 128), F32)
        for k, column in enumerate(columns):
            square = jnp.where(lane == k, column, square)
        self.held[0] = square.T[:8]
        self.groups[0].send(self.held.at[0], self.box.at[0], self.partner)

    def along_x(self):
        self.groups[0].received()
        self.held[1] = self.held[0] + self.box[0]
        for k, device in enumerate(self.x):
            self.groups[1].send(self.held.at[1], self.box.at[1 + k], device)

    def along_y(self):
        self.groups[1].received(self.box.at[pl.ds(1, 3)])
        self.held[2] = self.held[1] + self.box[1] + self.box[2] + self.box[3]
        for k, device in enumerate(self.y):
            self.groups[2].send(self.held.at[2], self.box.at[4 + k], device)

    def columns(self, count):
        self.groups[2].received(self.box.at[pl.ds(4, 3)])
        total = self.held[2] + self.box[4] + self.box[5] + self.box[6]
        square = jnp.concatenate([total, jnp.zeros((ROWS - 8, 128), F32)], axis=0).T
        return [square[:, k : k + 1] for k in range(count)]

    def sent(self):
        self.groups[0].sent()
        self.groups[1].sent(self.box.at[pl.ds(1, 3)])
        self.groups[2].sent(self.box.at[pl.ds(4, 3)])


def own_sums(block):
    values = block.astype(F32)
    return [jnp.sum(v, -1, keepdims=True) for v in (values, values * values)]


def statistics(total, square):
    center = total * (1.0 / D)
    return center, lax.rsqrt(square * (1.0 / D) - center * center + EPS)


def project(slots, gains, weights, total, center, inv_std, with_gain, first, last):
    def body(i, _):
        row, col = i % 4, (i // 4) * 2
        blocks = []
        for k in range(2):
            gain = gains[row, col + k]
            hidden = (slots[row, col + k].astype(F32) - center) * inv_std * gain
            block = hidden.astype(BF16)
            if with_gain:
                high = gain.astype(BF16).astype(F32)
                middle = (gain - high).astype(BF16).astype(F32)
                low = gain - high - middle
                at = lax.broadcasted_iota(jnp.int32, (16, WIDTH), 0)
                extra = jnp.where(at == 0, high, jnp.where(at == 1, middle, low))
                extra = jnp.where(at < 3, extra, 0.0)
                block = jnp.concatenate([block, extra.astype(BF16)], axis=0)
            blocks.append(block)
        lhs = jnp.concatenate(blocks, axis=1)
        rhs = weights[row, pl.ds(col, 2)].reshape(2 * WIDTH, 2 * THREE)
        value = mm(lhs, rhs)

        @pl.when(i == 0)
        def _():
            total[...] = value

        @pl.when(i > 0)
        def _():
            total[...] += value

        return 0

    lax.fori_loop(first, last, body, 0)


def visible_pairs(documents):
    across = jnp.broadcast_to(documents, (ROWS, ROWS))
    down = across.T
    query = lax.broadcasted_iota(jnp.int32, (ROWS, ROWS), 0)
    key = lax.broadcasted_iota(jnp.int32, (ROWS, ROWS), 1)
    return (key <= query) & (across == down)


def probabilities(queries, keys, visible):
    scores = jnp.where(visible, mm(queries, keys, NT) * SCALE, -1e30)
    exponent = jnp.exp(scores - jnp.max(scores, -1, keepdims=True))
    return exponent / jnp.sum(exponent, -1, keepdims=True)


def kernel(
    x_prev, x_saved, g_next, w_qkv, w_out, gain, documents,
    y_out, grad_out,
    sb, sg, sf, weights, w_o, gains, part_d, part_y,
    da1, da2, db1, db2, ya1, ya2, yb1, yb2,
    qkv_sum_b, qkv_sum_f, qkv_in, d_o, d_o_in, d_cat, o_cat,
    moments_held, moments_box, means_held, means_box, doc_ids,
    send_sems, recv_sems, local_sems, ready,
):
    z, t = lax.axis_index("pipe"), lax.axis_index("tp")
    core, x, y = t % 2, (t // 2) % 4, t // 8
    planes = lax.axis_size("pipe")

    def at(dy, dx):
        return (z, (((y + dy) % 4) * 4 + (x + dx) % 4) * 2 + core)

    partner = (z, t + 1 - 2 * core)
    above, below = ((z + 1) % planes, t), ((z + planes - 1) % planes, t)
    near = {"xp": at(0, 1), "xm": at(0, 3), "yp": at(1, 0), "ym": at(3, 0)}
    x_far, y_far = at(0, 2), at(2, 0)

    barrier = pltpu.get_barrier_semaphore()
    hello = functools.partial(pl.semaphore_signal, inc=1, device_id_type=MESH)
    on_plane = [at(0, 1), at(0, 2), at(0, 3), at(1, 0), at(2, 0), at(3, 0)]
    for device in on_plane:
        hello(barrier, device_id=(z, device[1] - core))
    for plane in (above, below):
        hello(barrier, device_id=(plane[0], t - core + 1))

    @pl.when(core == 1)
    def _():
        hello(barrier, device_id=partner)

    @pl.when(core == 0)
    def _():
        pl.semaphore_wait(barrier, 2 * len(on_plane) + 1)
        hello(ready.at[0], device_id=partner)

    @pl.when(core == 1)
    def _():
        pl.semaphore_wait(ready.at[0], 1)

    wire = Wire(send_sems, recv_sems, partner)
    gb, gf, gg = (Gather(wire, near, slots) for slots in (sb, sf, sg))
    rd = Scatter(wire, near, part_d, da1, da2, db1, db2)
    ry = Scatter(wire, near, part_y, ya1, ya2, yb1, yb2)
    on_x, on_y = (near["xp"], near["xm"], x_far), (near["yp"], near["ym"], y_far)
    moments = AllSum(wire, partner, on_x, on_y, moments_held, moments_box)
    means = AllSum(wire, partner, on_x, on_y, means_held, means_box)
    swap_w, swap_o = wire.group(), wire.group()
    own_cols, their_cols = pl.ds(0, THREE), pl.ds(THREE, THREE)
    own_rows, their_rows = pl.ds(0, HEAD_DIM), pl.ds(HEAD_DIM, HEAD_DIM)

    gb.first(x_saved)
    own_b = pltpu.make_async_copy(x_saved, sb.at[0, 0], local_sems.at[0])
    own_b.start()
    for py in range(4):
        for px in range(4):
            chip = ((y + OFFSET[py]) % 4) * 4 + (x + OFFSET[px]) % 4
            pltpu.make_async_copy(
                w_qkv.at[chip, core], weights.at[py, px, :, own_cols], local_sems.at[1]
            ).start()
            swap_w.send(w_qkv.at[chip, 1 - core], weights.at[py, px, :, their_cols], partner)
            pltpu.make_async_copy(
                gain.at[chip * 2 + core], gains.at[py, px], local_sems.at[3]
            ).start()
    @pl.when(core == 1)
    def _():
        pl.semaphore_wait(barrier, 4)
        hello(ready.at[1], device_id=partner)

    @pl.when(core == 0)
    def _():
        pl.semaphore_wait(ready.at[1], 1)

    shift_f = wire.send(x_prev, sf.at[0, 0], above)
    shift_g = wire.send(g_next, sg.at[0, 0], below)
    own_docs = pltpu.make_async_copy(documents, doc_ids, local_sems.at[4])
    own_docs.start()
    own_b.wait()
    gb.second()
    for py in range(4):
        for px in range(4):
            chip = ((y + OFFSET[py]) % 4) * 4 + (x + OFFSET[px]) % 4
            mine = pl.multiple_of((chip * 2 + core) * WIDTH, 128)
            theirs = pl.multiple_of((chip * 2 + 1 - core) * WIDTH, 128)
            pltpu.make_async_copy(
                w_out.at[:, pl.ds(mine, WIDTH)], w_o.at[py, px, own_rows], local_sems.at[2]
            ).start()
            swap_o.send(w_out.at[:, pl.ds(theirs, WIDTH)], w_o.at[py, px, their_rows], partner)
    gb.third()
    shift_f.received()
    gf.first(sf.at[0, 0])
    moments.start(own_sums(sb[0, 0]) + own_sums(sf[0, 0]))
    gb.fourth()
    moments.along_x()
    gf.second()
    gb.fifth()
    moments.along_y()
    gf.third()
    shift_g.received()
    gg.first(sg.at[0, 0])
    total_b, square_b, total_f, square_f = moments.columns(4)
    center_b, inv_std_b = statistics(total_b, square_b)
    center_f, inv_std_f = statistics(total_f, square_f)

    pltpu.make_async_copy(gains, gains, local_sems.at[3]).wait()
    half_w = weights.at[:, :, :, own_cols]
    pltpu.make_async_copy(half_w, half_w, local_sems.at[1]).wait()
    swap_w.received(weights.at[:, :, :, their_cols])
    own_docs.wait()

    def project_b(first, last):
        project(sb, gains, weights, qkv_sum_b, center_b, inv_std_b, True, first, last)

    def project_f(first, last):
        project(sf, gains, weights, qkv_sum_f, center_f, inv_std_f, False, first, last)

    project_b(0, 3)
    gb.finish()
    project_b(3, 6)
    gf.fourth()
    gf.fifth()
    gg.second()
    project_b(6, 8)
    trade_b = wire.send(qkv_sum_b.at[pl.ds(0, ROWS), their_cols], qkv_in.at[0], partner)
    project_f(0, 3)
    gg.third()
    gf.finish()
    project_f(3, 8)
    trade_f = wire.send(qkv_sum_f.at[:, their_cols], qkv_in.at[1], partner)

    trade_b.received()
    qkv_b = qkv_sum_b[pl.ds(0, ROWS), own_cols] + qkv_in[0]
    low_b = qkv_b.astype(BF16)
    queries_b, keys_b, values_b = (low_b[:, k * HEAD_DIM : (k + 1) * HEAD_DIM] for k in range(3))
    probs_b = probabilities(queries_b, keys_b, visible_pairs(doc_ids[pl.ds(1, 1)]))
    gg.fourth()

    trade_f.received()
    low_f = (qkv_sum_f[:, own_cols] + qkv_in[1]).astype(BF16)
    queries, keys, values = (low_f[:, k * HEAD_DIM : (k + 1) * HEAD_DIM] for k in range(3))
    probs = probabilities(queries, keys, visible_pairs(doc_ids[pl.ds(0, 1)]))
    o_cat[:, own_rows] = mm(probs.astype(BF16), values).astype(BF16)
    trade_o = wire.send(o_cat.at[:, own_rows], o_cat.at[:, their_rows], partner)
    gg.fifth()
    half_o = w_o.at[:, :, own_rows]
    pltpu.make_async_copy(half_o, half_o, local_sems.at[2]).wait()
    swap_o.received(w_o.at[:, :, their_rows])

    def output_gradient(i, total):
        row, col = i % 4, (i // 4) * 2
        lhs = jnp.concatenate([sg[row, col], sg[row, col + 1]], axis=1)
        rhs = jnp.concatenate([w_o[row, col], w_o[row, col + 1]], axis=1)
        return total + mm(lhs, rhs, NT)

    d_o[...] = lax.fori_loop(0, 3, output_gradient, jnp.zeros((ROWS, 2 * HEAD_DIM), F32))
    trade_o.received()
    o_all = o_cat[...]

    def output_blocks(py, px):
        rhs = jnp.concatenate([w_o[py, px], w_o[py, px + 1]], axis=1)
        value = mm(o_all, rhs).astype(BF16)
        part_y[py, px] = value[:, :WIDTH]
        part_y[py, px + 1] = value[:, WIDTH:]

    def scatter(reduction, blocks):
        blocks(3, 2)
        reduction.far(0, 0)
        reduction.far(0, 1)
        blocks(1, 2)
        blocks(2, 2)
        reduction.close(0, 0)
        reduction.far(1, 1)
        blocks(3, 0)
        reduction.close(0, 1)
        reduction.far(1, 0)
        blocks(0, 2)
        reduction.far(2, 0)
        reduction.far(2, 1)
        blocks(1, 0)
        blocks(2, 0)
        reduction.close(1, 0)
        reduction.close(1, 1)
        reduction.close(2, 0)
        blocks(0, 0)
        reduction.close(2, 1)

    scatter(ry, output_blocks)

    gg.finish()

    d_o[...] = lax.fori_loop(3, 8, output_gradient, d_o[...])
    trade_d = wire.send(d_o.at[:, their_rows], d_o_in, partner)
    probs_low = probs_b.astype(BF16)
    ry.second(0)
    trade_d.received()
    d_low = (d_o[:, own_rows] + d_o_in[...]).astype(BF16)
    d_values = mm(probs_low, d_low, TN).astype(BF16)
    d_probs = mm(d_low, values_b, NT)
    d_scores = probs_b * (d_probs - jnp.sum(d_probs * probs_b, -1, keepdims=True)) * SCALE
    d_scores = d_scores.astype(BF16)
    d_queries = mm(d_scores, keys_b).astype(BF16)
    d_keys = mm(d_scores, queries_b, TN).astype(BF16)
    d_own = jnp.concatenate([d_queries, d_keys, d_values], axis=1)
    d_cat[:, own_cols] = d_own
    trade_c = wire.send(d_cat.at[:, own_cols], d_cat.at[:, their_cols], partner)
    ry.second(1)
    along_qkv = jnp.sum(d_own.astype(F32) * qkv_b, -1, keepdims=True)
    trade_c.received()

    d_all = d_cat[...]

    def input_blocks(py, px):
        rhs = weights[py, pl.ds(px, 2)].reshape(2 * WIDTH, 2 * THREE)
        value = mm(d_all, rhs, NT).astype(BF16)
        part_d[py, px] = value[:, :WIDTH]
        part_d[py, px + 1] = value[:, WIDTH:]

    scatter(rd, input_blocks)
    ry.second(2)

    gain_w = jnp.sum(qkv_sum_b[pl.ds(ROWS, 8)], 0, keepdims=True)
    along_gain = jnp.sum(d_all.astype(F32) * gain_w, -1, keepdims=True)
    means.start([along_gain, along_qkv])
    ry.third()
    rd.second(0)
    means.along_x()
    ry.fourth()
    rd.second(1)
    ry.fifth()
    means.along_y()
    rd.second(2)
    rd.third()
    y_out[...] = (sf[0, 0].astype(F32) + ry.finish()).astype(BF16)
    rd.fourth()
    mean_d, mean_dx = means.columns(2)
    x_hat = (sb[0, 0].astype(F32) - center_b) * inv_std_b
    rest = sg[0, 0].astype(F32) - inv_std_b * (mean_d + x_hat * mean_dx) * (1.0 / D)
    rd.fifth()
    all_sent = weights.at[:, 0, pl.ds(0, 240)]
    for one in (gb, gf, gg, ry):
        Group(one.sender, None, partner).sent(all_sent)
    for one in (
        shift_f, shift_g, trade_b, trade_f, trade_o, trade_d, trade_c, moments, means
    ):
        one.sent()
    swap_w.sent(weights.at[:, :, :, their_cols])
    swap_o.sent(w_o.at[:, :, their_rows])
    grad_out[...] = (rest + inv_std_b * (rd.finish() * gains[0, 0])).astype(BF16)
    Group(rd.sender, None, partner).sent(all_sent)


def place(y_ref, grad_ref, y_out, grad_out, sems):
    copies = [
        pltpu.make_async_copy(y_ref, y_out, sems.at[0]),
        pltpu.make_async_copy(grad_ref, grad_out, sems.at[1]),
    ]
    for copy in copies:
        copy.start()
    for copy in copies:
        copy.wait()


def shards(x_prev, x_saved, g_next, w_qkv, w_out, gain, doc_ids):
    block = (ROWS, WIDTH)
    grid = (4, 4)
    any_spec = pl.BlockSpec(memory_space=pl.ANY)
    vmem_spec = pl.BlockSpec(memory_space=pltpu.VMEM)
    scatter_space = [
        pltpu.VMEM((2, 2, 4, QUARTER, WIDTH), BF16),
        pltpu.VMEM((2, 2, 4, HALF, WIDTH), BF16),
        pltpu.VMEM((2, 2, QUARTER, WIDTH), BF16),
        pltpu.VMEM((2, 2, HALF, WIDTH), BF16),
    ]
    y_out, grad = pl.pallas_call(
        kernel,
        out_shape=[jax.ShapeDtypeStruct(block, BF16)] * 2,
        in_specs=[any_spec] * 7,
        out_specs=[vmem_spec] * 2,
        scratch_shapes=[
            *[pltpu.VMEM(grid + block, BF16)] * 3,
            pltpu.VMEM(grid + (WIDTH, 2 * THREE), BF16),
            pltpu.VMEM(grid + (2 * HEAD_DIM, WIDTH), BF16),
            pltpu.VMEM(grid + (1, WIDTH), F32),
            *[pltpu.VMEM(grid + block, BF16)] * 2,
            *scatter_space,
            *scatter_space,
            pltpu.VMEM((ROWS + 16, 2 * THREE), F32),
            pltpu.VMEM((ROWS, 2 * THREE), F32),
            pltpu.VMEM((2, ROWS, THREE), F32),
            pltpu.VMEM((ROWS, 2 * HEAD_DIM), F32),
            pltpu.VMEM((ROWS, HEAD_DIM), F32),
            pltpu.VMEM((ROWS, 2 * THREE), BF16),
            pltpu.VMEM((ROWS, 2 * HEAD_DIM), BF16),
            *[pltpu.VMEM((3, 8, 128), F32), pltpu.VMEM((7, 8, 128), F32)] * 2,
            pltpu.VMEM((2, ROWS), jnp.int32),
            pltpu.SemaphoreType.DMA((N_SENDERS,)),
            pltpu.SemaphoreType.DMA((N_RECEIVERS,)),
            pltpu.SemaphoreType.DMA((5,)),
            pltpu.SemaphoreType.REGULAR((2,)),
        ],
        compiler_params=pltpu.CompilerParams(
            collective_id=0, has_side_effects=True, vmem_limit_bytes=56 * 2**20
        ),
        name="section",
    )(
        x_prev[0],
        x_saved[0],
        g_next[0],
        w_qkv.reshape(16, 2, WIDTH, THREE),
        w_out[0],
        gain.reshape(32, 1, WIDTH),
        doc_ids[0],
    )
    y_out, grad = pl.pallas_call(
        place,
        out_shape=[jax.ShapeDtypeStruct(block, BF16)] * 2,
        in_specs=[vmem_spec] * 2,
        out_specs=[any_spec] * 2,
        scratch_shapes=[pltpu.SemaphoreType.DMA((2,))],
        name="place",
    )(y_out, grad)
    return y_out[None], grad[None]


def solution(mesh):
    in_specs = (
        P("pipe", None, "tp"),
        P("pipe", None, "tp"),
        P("pipe", None, "tp"),
        P("pipe", None, "tp", None),
        P("pipe", "tp", None),
        P("pipe", None),
        P("pipe", None, None),
    )
    out_specs = (P("pipe", None, "tp"), P("pipe", None, "tp"))
    return jax.shard_map(shards, mesh=mesh, in_specs=in_specs, out_specs=out_specs, check_vma=False)
```
